256 devices in a mesh: view: 32 (over z_lo, y, core), head: 4 (over x), branch: 2 (over z_hi).
Axes of the slice: x: 4, y: 4, z: 8 (z_hi: 2, z_lo: 4; z = z_hi * 4 + z_lo), core: 2. Of those that a mesh axis runs over, the one named last changes fastest.
Arguments:
- tokens: bfloat16 [2, 64, 128, 1024], P('branch', 'view'), may hold values from -14 to 14
- partners: int32 [8, 64], P(None, 'view'), may hold values from 0 to 63, as said below
- counts: int32 [64], P('view'), may hold values from 4 to 8
- w_query: bfloat16 [1024, 1024], P(None, 'head'), may hold values from -1 to 1
- w_key: bfloat16 [1024, 1024], P(None, 'head'), may hold values from -1 to 1
- w_value: bfloat16 [1024, 1024], P(None, 'head'), may hold values from -0.75 to 0.75
- w_out: bfloat16 [1024, 1024], P('head'), may hold values from -0.75 to 0.75
- w_in: bfloat16 [1024, 4096], P(None, 'head'), may hold values from -0.1875 to 0.1875
- w_back: bfloat16 [4096, 1024], P('head'), may hold values from -0.09375 to 0.09375
- guidance: float32 [1], replicated, may hold values from 2 to 6
Outputs:
- guided: bfloat16 [64, 128, 1024], P('view', ('head', 'branch'))
The draws below stay inside these ranges and needn't reach their ends.
Inputs may be any that keep to these rules, and one draw needn't show every extreme that they name: In each round the views are paired: partners[r, partners[r, v]] = v and partners[r, v] != v; the two views of a pair lie a cyclic distance apart that is a power of two up to 8, the same for all pairs of the round; each such distance is taken by one of the first rounds.
All inputs are finite; a program needn't handle non-finite values.
Results may differ from the reference program's by a relative error of at most 0.022.
Values may be sent and summed in bfloat16 or wider, within the bound.
No kernel may reach another device: no remote copies, remote signals or barrier semaphores. Data moves between devices by JAX's collectives and lax.ppermute only.
A program may use at most 64 MiB of HBM per device.

```python
import math
import jax
import jax.numpy as jnp
from jax import lax

D = 1024
HEADS = 16
HD = 64
FF = 4096
TOK = 128
ROUNDS = 8
HOP_MAX = 8
VIEWS = 64
N_HEAD = 4
N_BRANCH = 2


def draw_w_query(key, part):
    key = jax.random.fold_in(key, 21)
    return (jnp.clip(jax.random.normal(key, (D, D), jnp.float32), -6.0, 6.0) * D ** (-0.5)).astype(jnp.bfloat16)


def draw_w_key(key, part):
    key = jax.random.fold_in(key, 22)
    return (jnp.clip(jax.random.normal(key, (D, D), jnp.float32), -6.0, 6.0) * D ** (-0.5)).astype(jnp.bfloat16)


def draw_tokens(key, part):
    key = jax.random.fold_in(key, 23)
    array_shape = (N_BRANCH, VIEWS, TOK, D)
    return jnp.clip(jax.random.normal(key, array_shape, jnp.float32), -6.0, 6.0).astype(jnp.bfloat16)


def draw_partners(key, part):
    key = jax.random.fold_in(key, 24)
    key_order, key_pick, key_offset = jax.random.split(key, 3)
    largest = min(HOP_MAX, VIEWS // 2)
    number = largest.bit_length()
    hop_sizes = (2 ** jnp.arange(number)).astype(jnp.int32)
    opening = jax.random.permutation(key_order, hop_sizes)
    later = hop_sizes[jax.random.randint(key_pick, (ROUNDS - number,), 0, number)]
    round_hops = jnp.concatenate([opening, later]).astype(jnp.int32)
    offsets = jax.random.randint(key_offset, (ROUNDS,), 0, VIEWS).astype(jnp.int32)
    view_ids = jnp.arange(VIEWS, dtype=jnp.int32)
    shifted = (view_ids[None, :] - offsets[:, None]) % VIEWS
    paired = jnp.bitwise_xor(shifted, round_hops[:, None])
    return ((paired + offsets[:, None]) % VIEWS).astype(jnp.int32)


def set_ends(values, rng, least, high):
    index_at = [jax.random.randint(jax.random.fold_in(rng, axis), (), 0, length) for axis, length in enumerate(values.shape)]
    longest = values.shape.index(max(values.shape))
    next_to = index_at[:longest] + [(index_at[longest] + 1) % values.shape[longest]] + index_at[longest + 1:]
    return values.at[tuple(index_at)].set(least).at[tuple(next_to)].set(high)


def shard_levels(rng, shape, cuts, low, high):
    loudness, own = 1.0, jax.random.fold_in(rng, 6)
    for position, blocks in cuts:
        steps = jnp.exp(jax.random.uniform(jax.random.fold_in(own, position), (blocks,), jnp.float32, low / len(cuts), high / len(cuts)))
        loudness = loudness * jnp.repeat(steps, shape[position] // blocks).reshape([-1 if axis == position else 1 for axis in range(len(shape))])
    return loudness


def normal_values(key, extent, deviation, limit, shards=(), held_as=jnp.bfloat16):
    loudness = shard_levels(key, extent, shards, -0.22, 0.18) if shards else 1.0
    entries = jax.random.normal(key, extent, jnp.float32) * deviation * loudness
    return jnp.minimum(jnp.maximum(entries, -limit), limit).astype(held_as)


def setup_inputs(seed: int = 0) -> dict:
    streams_of = jax.random.split(jax.random.key(seed), 11)
    tokens = draw_tokens(jax.random.fold_in(streams_of[10], 71), 0)
    partners = draw_partners(jax.random.fold_in(streams_of[10], 71), 0)
    counts = set_ends(jax.random.randint(streams_of[2], (VIEWS,), 4, ROUNDS + 1), jax.random.fold_in(streams_of[2], 1), 4, ROUNDS).astype(jnp.int32)
    w_query = draw_w_query(jax.random.fold_in(streams_of[10], 71), 0)
    w_key = draw_w_key(jax.random.fold_in(streams_of[10], 71), 0)
    w_value = normal_values(streams_of[5], (D, D), HD ** -0.5, 0.75, ((1, 4),))
    w_out = normal_values(streams_of[6], (D, D), HD ** -0.5, 0.75, ((0, 4),))
    w_in = normal_values(streams_of[7], (D, FF), D ** -0.5, 0.1875, ((1, 4),))
    w_back = normal_values(streams_of[8], (FF, D), FF ** -0.5, 0.09375, ((0, 4),))
    guidance = jnp.clip(jnp.exp(jax.random.uniform(streams_of[9], (1,), jnp.float32, math.log(2.0), math.log(6.0))), 2.0, 6.0)
    return {"tokens": tokens, "partners": partners, "counts": counts, "w_query": w_query, "w_key": w_key, "w_value": w_value, "w_out": w_out, "w_in": w_in, "w_back": w_back, "guidance": guidance}


masked_score = -1e+30

def rms_rows(values):
    return values * lax.rsqrt(lax.optimization_barrier(jnp.mean(values * values, axis=-1, keepdims=True)) + 1e-06)

def reference(tokens, partners, counts, w_query, w_key, w_value, w_out, w_in, w_back, guidance):
    flat_rows = tokens.reshape(N_BRANCH * VIEWS * TOK, D)
    all_keys = jnp.dot(flat_rows, w_key, preferred_element_type=jnp.float32).astype(jnp.bfloat16).reshape(N_BRANCH, VIEWS, TOK, HEADS, HD)
    all_values = jnp.dot(flat_rows, w_value, preferred_element_type=jnp.float32).astype(jnp.bfloat16).reshape(N_BRANCH, VIEWS, TOK, HEADS, HD)
    round_ids = jnp.arange(ROUNDS, dtype=jnp.int32)
    w_parts = w_out.reshape(N_HEAD, D // N_HEAD, D).astype(jnp.float32)

    def one_view(view_item):
        branch_id = view_item[0]
        view_id = view_item[1]
        view_tokens = tokens[branch_id, view_id]
        queries = (jnp.dot(view_tokens, w_query, preferred_element_type=jnp.float32) * HD ** (-0.5)).astype(jnp.bfloat16).reshape(TOK, HEADS, HD)
        chosen = jnp.concatenate([view_id[None], partners[:, view_id]]).astype(jnp.int32)
        active = jnp.concatenate([jnp.ones((1,), dtype=bool), round_ids < counts[view_id]])
        near_keys = all_keys[branch_id][chosen]
        near_values = all_values[branch_id][chosen]
        scores = jnp.einsum('qhd,rkhd->hqrk', queries.astype(jnp.float32), near_keys.astype(jnp.float32))
        scores = jnp.where(active[None, None, :, None], scores, masked_score)
        largest = lax.optimization_barrier(jnp.max(scores, axis=(2, 3), keepdims=True))
        weights = jnp.exp(scores - largest)
        denominator = lax.optimization_barrier(jnp.sum(weights, axis=(2, 3)))
        rounded = lax.optimization_barrier(weights.astype(jnp.bfloat16))
        blended = jnp.einsum('hqrk,rkhd->qhd', rounded.astype(jnp.float32), near_values.astype(jnp.float32))
        attended = (blended / denominator.T[:, :, None]).astype(jnp.bfloat16).reshape(TOK, N_HEAD, D // N_HEAD)
        partial_sums = lax.optimization_barrier(jnp.einsum('tgc,gcd->gtd', attended.astype(jnp.float32), w_parts).astype(jnp.bfloat16))
        attention = lax.optimization_barrier(jnp.sum(partial_sums.astype(jnp.float32), axis=0))
        normed = rms_rows(view_tokens.astype(jnp.float32) + attention).astype(jnp.bfloat16)
        hidden = jax.nn.gelu(jnp.dot(normed, w_in, preferred_element_type=jnp.float32)).astype(jnp.bfloat16)
        return attention + jnp.dot(hidden, w_back, preferred_element_type=jnp.float32)
    view_items = jnp.stack([jnp.repeat(jnp.arange(N_BRANCH), VIEWS), jnp.tile(jnp.arange(VIEWS), N_BRANCH)], axis=1).astype(jnp.int32)
    updates = lax.map(one_view, view_items).reshape(N_BRANCH, VIEWS, TOK, D)
    strength = guidance[0]
    return (updates[1] + strength * (updates[0] - updates[1])).astype(jnp.bfloat16)
```

```python
import functools

import jax
import jax.numpy as jnp
from jax import lax
from jax.experimental import pallas as pl
from jax.experimental.pallas import tpu as pltpu
from jax.sharding import PartitionSpec as P

HD = 64
ROUNDS = 8
MASKED = -1e30

NT = (((1,), (1,)), ((), ()))
VMEM = pl.BlockSpec(memory_space=pltpu.VMEM)
SMEM = pl.BlockSpec(memory_space=pltpu.SMEM)
ANY = pl.BlockSpec(memory_space=pl.ANY)


def params(mib):
    return pltpu.CompilerParams(vmem_limit_bytes=mib * 1024 * 1024)


def matched(axis, count, apart, parity):
    route = []
    for low in range(count):
        if (low // apart) % 2 == parity:
            high = (low + apart) % count
            route += [(low, high), (high, low)]
    return functools.partial(lax.ppermute, axis_name=axis, perm=route)


def flipped(axis, count, bits):
    return functools.partial(lax.ppermute, axis_name=axis, perm=[(i, i ^ bits) for i in range(count)])


def dot(a, b):
    return jnp.dot(a, b, preferred_element_type=jnp.float32)


def project_kernel(x_ref, wq_ref, wk_ref, wv_ref, q_ref, kv_ref):
    x = x_ref[...]
    q = (dot(x, wq_ref[...]) * HD ** (-0.5)).astype(jnp.bfloat16)
    k = dot(x, wk_ref[...]).astype(jnp.bfloat16)
    v = dot(x, wv_ref[...]).astype(jnp.bfloat16)
    zeros = jnp.zeros((x.shape[0], HD), jnp.bfloat16)
    for h in range(q_ref.shape[0]):
        cols = slice(h * HD, (h + 1) * HD)
        q_ref[h] = jnp.concatenate([q[:, cols], zeros], axis=1)
        kv_ref[h] = jnp.concatenate([k[:, cols], v[:, cols]], axis=1)


def project(x, w_query, w_key, w_value):
    rows, width = x.shape
    heads = w_query.shape[1] // HD
    shape = jax.ShapeDtypeStruct((heads, rows, 2 * HD), jnp.bfloat16)
    return pl.pallas_call(
        project_kernel,
        out_shape=(shape, shape),
        in_specs=[VMEM] * 4,
        out_specs=(VMEM, VMEM),
        compiler_params=params(32),
        cost_estimate=pl.CostEstimate(flops=6 * rows * width * heads * HD, bytes_accessed=3_000_000, transcendentals=0),
        name="project",
    )(x, w_query, w_key, w_value)


def attend_kernel(blocks, first, last, bias_ref, q_ref, *refs):
    count = len(blocks)
    kv_refs = refs[:count]
    state_ref = None if first else refs[count]
    out_ref = refs[-1]
    heads, rows, _ = q_ref.shape
    tok = rows // 2
    for qv in range(2):
        for h in range(heads):
            q = q_ref[h, qv * tok : (qv + 1) * tok, :]
            scores, taken = [], []
            for (slot, both), kv_ref in zip(blocks, kv_refs):
                for kvw in (0, 1) if both else (qv,):
                    kv = kv_ref[h, kvw * tok : (kvw + 1) * tok, :]
                    s = lax.dot_general(q, kv, NT, preferred_element_type=jnp.float32)
                    scores.append(s + bias_ref[qv, 2 * slot + kvw])
                    taken.append(kv)
            top = functools.reduce(jnp.maximum, scores)
            top = jnp.max(top, axis=1, keepdims=True)
            if not first:
                held = state_ref[qv * heads + h]
                old_top, old_sum = held[:, 0:1], held[:, 1:2]
                top = jnp.maximum(top, old_top)
            weights = [jnp.exp(s - top) for s in scores]
            total = jnp.sum(functools.reduce(jnp.add, weights), axis=1, keepdims=True)
            blended = dot(jnp.concatenate([w.astype(jnp.bfloat16) for w in weights], axis=1), jnp.concatenate(taken, axis=0))
            if not first:
                scale = jnp.exp(old_top - top)
                total = total + scale * old_sum
                blended = blended + scale * held
            if last:
                done = blended[:, HD:] / total
                out_ref[qv * tok : (qv + 1) * tok, h * HD : (h + 1) * HD] = done.astype(jnp.bfloat16)
            else:
                lane = lax.broadcasted_iota(jnp.int32, blended.shape, 1)
                kept = jnp.where(lane == 0, top, jnp.where(lane == 1, total, blended))
                out_ref[qv * heads + h] = kept


def attend(blocks, first, last, bias, q, kvs, state=None):
    heads, rows, _ = q.shape
    tok = rows // 2
    if last:
        out = jax.ShapeDtypeStruct((rows, heads * HD), jnp.bfloat16)
    else:
        out = jax.ShapeDtypeStruct((2 * heads, tok, 2 * HD), jnp.float32)
    pairs = sum(4 if both else 2 for _, both in blocks)
    held = () if first else (state,)
    return pl.pallas_call(
        functools.partial(attend_kernel, blocks, first, last),
        out_shape=out,
        in_specs=[SMEM] + [VMEM] * (1 + len(kvs) + len(held)),
        out_specs=VMEM,
        compiler_params=params(32),
        cost_estimate=pl.CostEstimate(
            flops=pairs * heads * tok * tok * 8 * HD, bytes_accessed=1_000_000, transcendentals=pairs * heads * tok * tok
        ),
        name="attend",
    )(bias, q, *kvs, *held)


def feed_kernel(head_ref, x_ref, a0, a1, a2, a3, o0, o1, o2, o3, win_hbm, wback_hbm, own_ref, r1, r2, r3, win, wback, sems):
    load_in = pltpu.make_async_copy(win_hbm, win, sems.at[0])
    load_back = pltpu.make_async_copy(wback_hbm, wback, sems.at[1])
    load_in.start()
    load_back.start()
    head = head_ref[0]
    rows, width = x_ref.shape
    tok = rows // 2
    part = tok // 4

    def turned(ref):
        pieces = []
        for j in range(4):
            for view in range(2):
                start = pl.multiple_of(view * tok + jnp.bitwise_xor(head, j) * part, part)
                pieces.append(ref[pl.ds(start, part), :])
        return jnp.concatenate(pieces, axis=0)

    attention = dot(turned(a0), o0[...])
    for a, o in ((a1, o1), (a2, o2), (a3, o3)):
        attention = attention + dot(turned(a), o[...])
    y = turned(x_ref).astype(jnp.float32) + attention
    normed = (y * lax.rsqrt(jnp.mean(y * y, axis=-1, keepdims=True) + 1e-06)).astype(jnp.bfloat16)
    load_in.wait()
    hidden = jax.nn.gelu(dot(normed, win[...])).astype(jnp.bfloat16)
    load_back.wait()
    update = dot(hidden, wback[...])
    own_ref[...] = attention[: 2 * part] + update[: 2 * part]
    for j, ref in ((1, r1), (2, r2), (3, r3)):
        ref[...] = update[2 * part * j : 2 * part * (j + 1)].astype(jnp.bfloat16)


def feed(head, x, attended, w_outs, w_in, w_back):
    rows, width = x.shape
    piece = jax.ShapeDtypeStruct((rows // 4, width), jnp.bfloat16)
    return pl.pallas_call(
        feed_kernel,
        out_shape=(jax.ShapeDtypeStruct((rows // 4, width), jnp.float32), piece, piece, piece),
        in_specs=[SMEM] + [VMEM] * 9 + [ANY, ANY],
        out_specs=(VMEM,) * 4,
        scratch_shapes=[
            pltpu.VMEM(w_in.shape, jnp.bfloat16),
            pltpu.VMEM(w_back.shape, jnp.bfloat16),
            pltpu.SemaphoreType.DMA((2,)),
        ],
        compiler_params=params(40),
        cost_estimate=pl.CostEstimate(flops=6 * rows * width * width, bytes_accessed=8_000_000, transcendentals=rows * width),
        name="feed",
    )(head, x, *attended, *w_outs, w_in, w_back)


def gather_kernel(branch_ref, own_ref, r1, r2, r3, kept_ref, sent_ref):
    branch = branch_ref[0]
    part = own_ref.shape[0] // 2
    half = part // 2
    for view in range(2):
        for side, ref in ((branch, kept_ref), (1 - branch, sent_ref)):
            rows = pl.ds(pl.multiple_of(view * part + side * half, half), half)
            total = own_ref[rows, :]
            for r in (r1, r2, r3):
                total = total + r[rows, :].astype(jnp.float32)
            ref[view * half : (view + 1) * half, :] = total.astype(ref.dtype)


def gather(branch, own, received):
    rows, width = own.shape
    return pl.pallas_call(
        gather_kernel,
        out_shape=(
            jax.ShapeDtypeStruct((rows // 2, width), jnp.float32),
            jax.ShapeDtypeStruct((rows // 2, width), jnp.bfloat16),
        ),
        in_specs=[SMEM] + [VMEM] * 4,
        out_specs=(VMEM, VMEM),
        name="gather",
    )(branch, own, *received)


def on_device(tokens, partners, counts, w_query, w_key, w_value, w_out, w_in, w_back, guidance):
    per_device, tok, width = tokens.shape[1:]
    x = tokens[0].reshape(per_device * tok, width)
    count = lax.axis_size("view")
    me = lax.axis_index("view")
    head = lax.axis_index("head").astype(jnp.int32)
    branch = lax.axis_index("branch").astype(jnp.int32)

    q, kv = project(x, w_query, w_key, w_value)

    chip_odd, pair_odd, core = (me // 2) % 2, (me // 4) % 2, me % 2
    near_a, near_b = me + 2 - 4 * chip_odd, me - 2 + 4 * chip_odd
    far_a, far_b = me + 4 - 8 * pair_odd, me - 4 + 8 * pair_odd
    sources = jnp.stack([me, me + 1 - 2 * core, near_a, near_b, me - 1 + 2 * core, far_a, far_b]) % count
    key_views = (sources[:, None] * per_device + jnp.arange(per_device)[None, :]).reshape(-1)
    active = jnp.arange(ROUNDS, dtype=jnp.int32)[:, None] < counts[None, :]
    matches = (partners[:, :, None] == key_views[None, None, :]) & active[:, :, None]
    own_views = me * per_device + jnp.arange(per_device)
    times = jnp.sum(matches.astype(jnp.float32), axis=0) + (own_views[:, None] == key_views[None, :])
    bias = jnp.where(times > 0, jnp.log(jnp.maximum(times, 1.0)), MASKED).astype(jnp.float32)

    sibling = matched("view", count, 1, 0)
    kv_sibling = sibling(kv)
    kv_near_a = matched("view", count, 2, 0)(kv)
    kv_near_b = matched("view", count, 2, 1)(kv)
    kv_far_a = matched("view", count, 4, 0)(kv)
    kv_far_b = matched("view", count, 4, 1)(kv)
    kv_cross = sibling(jnp.where((chip_odd + core) % 2 == 0, kv_near_a, kv_near_b))

    w_1 = flipped("head", 4, 1)(w_out)
    w_32 = flipped("head", 4, 3)(jnp.stack([w_out, w_1]))
    w_outs = (w_out, w_1, w_32[1], w_32[0])

    state = attend(((0, True), (1, True)), True, False, bias, q, (kv, kv_sibling))
    state = attend(((2, False), (3, False), (4, True)), False, False, bias, q, (kv_near_a, kv_near_b, kv_cross), state)
    attended = attend(((5, False), (6, False)), False, True, bias, q, (kv_far_a, kv_far_b), state)

    pieces = [attended] + [flipped("head", 4, j)(attended) for j in (1, 2, 3)]
    own, *outgoing = feed(head[None], x, pieces, w_outs, w_in, w_back)
    received = [flipped("head", 4, j)(r) for j, r in zip((1, 2, 3), outgoing)]
    kept, sent = gather(branch[None], own, received)
    other = flipped("branch", 2, 1)(sent)
    strength = guidance[0]
    weight = jnp.where(branch == 0, strength, 1.0 - strength)
    guided = weight * kept + (1.0 - weight) * other.astype(jnp.float32)
    return guided.reshape(per_device, -1, width).astype(jnp.bfloat16)


def solution(mesh):
    placed = (
        P("branch", "view", None, None),
        P(None, "view"),
        P("view"),
        P(None, "head"),
        P(None, "head"),
        P(None, "head"),
        P("head", None),
        P(None, "head"),
        P("head", None),
        P(),
    )
    return jax.shard_map(
        on_device,
        mesh=mesh,
        in_specs=placed,
        out_specs=P("view", ("head", "branch"), None),
        check_vma=False,
    )
```

```python
import functools

import jax
import jax.numpy as jnp
from jax import lax
from jax.experimental import pallas as pl
from jax.experimental.pallas import tpu as pltpu
from jax.sharding import PartitionSpec as P

HD = 64
ROUNDS = 8
BIASES = 16
DIAGONAL = (2, 3, 5, 6)
MASKED = -1e30
LOG2E = 1.4426950408889634

NT = (((1,), (1,)), ((), ()))
VMEM = pl.BlockSpec(memory_space=pltpu.VMEM)
SMEM = pl.BlockSpec(memory_space=pltpu.SMEM)
HBM = pl.BlockSpec(memory_space=pltpu.HBM)
ANY = pl.BlockSpec(memory_space=pl.ANY)


def params(mib):
    return pltpu.CompilerParams(vmem_limit_bytes=int(mib * 1024 * 1024))


def shifted(axis, count, apart):
    return functools.partial(lax.ppermute, axis_name=axis, perm=[(i, (i - apart) % count) for i in range(count)])


def flipped(axis, count, bits):
    return functools.partial(lax.ppermute, axis_name=axis, perm=[(i, i ^ bits) for i in range(count)])


def held(shape, dtype):
    return pltpu.VMEM(shape, dtype)


def outside(*arrays):
    return tuple(pltpu.with_memory_space_constraint(a, pltpu.HBM) for a in arrays)


COST = pl.CostEstimate(flops=1000, bytes_accessed=1000, transcendentals=0)


def dot(a, b):
    return jnp.dot(a, b, preferred_element_type=jnp.float32)


def chunked(source, target, sems, count):
    rows = source.shape[0] // count
    pieces = [pl.ds(i * rows, rows) for i in range(count)]
    return [pltpu.make_async_copy(source.at[p], target.at[p], sems.at[i]) for i, p in enumerate(pieces)]


def key_views(count):
    me = lax.axis_index("view")
    core = me & 1
    sources = (me, me + 1 - 2 * core, me + 2, me - 2, me - 1 + 2 * core, me + 4, me - 4)
    return [2 * lax.rem(s + count, count) for s in sources]


def bias_kernel(count, partners_ref, counts_ref, bias_ref):
    bias_ref[...] = jnp.zeros_like(bias_ref)
    firsts = key_views(count)
    for qv in range(2):
        used = counts_ref[qv]
        named = [jnp.where(r < used, partners_ref[qv, r], -1) for r in range(ROUNDS)]
        for slot, first in enumerate(firsts):
            for kvw in range(2):
                if (slot in DIAGONAL or slot == 0) and (kvw == qv) == (slot == 0):
                    continue
                times = sum((n == first + kvw).astype(jnp.int32) for n in named)
                row = BIASES * qv + 2 * slot + kvw
                bias_ref[row : row + 1] = jnp.full((1, bias_ref.shape[1]), times.astype(jnp.float32))
    times = bias_ref[...]
    bias_ref[...] = jnp.where(times > 0, jnp.log2(jnp.maximum(times, 1.0)), MASKED)
    for qv in range(2):
        row = BIASES * qv + qv
        bias_ref[row : row + 1] = jnp.zeros((1, bias_ref.shape[1]), jnp.float32)


def biases(count, partners, counts):
    return pl.pallas_call(
        functools.partial(bias_kernel, count),
        out_shape=held((2 * BIASES, 2 * HD), jnp.float32),
        in_specs=[SMEM, SMEM],
        out_specs=VMEM,
        compiler_params=params(2),
        cost_estimate=COST,
        name="biases",
    )(partners, counts)


def project_kernel(x_hbm, wk_hbm, wv_hbm, wq_hbm, q_ref, kv_ref, x, wk, wv, wq, sems):
    loads = [
        chunked(source, target, sems.at[i], sems.shape[1])
        for i, (source, target) in enumerate(((x_hbm, x), (wk_hbm, wk), (wv_hbm, wv), (wq_hbm, wq)))
    ]
    for copies in loads:
        for copy in copies:
            copy.start()

    def arrived(i):
        for copy in loads[i]:
            copy.wait()

    rows = x.shape[0]
    arrived(0)
    arrived(1)
    kv_ref[:rows] = dot(x[...], wk[...]).astype(jnp.bfloat16)
    arrived(2)
    kv_ref[rows:] = dot(x[...], wv[...]).T.astype(jnp.bfloat16)
    arrived(3)
    q_ref[...] = (dot(x[...], wq[...]) * (HD ** (-0.5) * LOG2E)).astype(jnp.bfloat16)


def project(x, w_query, w_key, w_value):
    rows, width = x.shape
    columns = w_query.shape[1]
    chunks = 1
    return pl.pallas_call(
        project_kernel,
        out_shape=(
            held((rows, columns), jnp.bfloat16),
            held((rows + columns, rows), jnp.bfloat16),
        ),
        in_specs=[HBM] * 4,
        out_specs=(VMEM, VMEM),
        scratch_shapes=[pltpu.VMEM(x.shape, jnp.bfloat16)]
        + [pltpu.VMEM((width, columns), jnp.bfloat16)] * 3
        + [pltpu.SemaphoreType.DMA((4, chunks))],
        compiler_params=params(8),
        cost_estimate=COST,
        name="project",
    )(*outside(x, w_key, w_value, w_query))


def attend_kernel(blocks, first, last, bias_ref, q_ref, *refs):
    count = len(blocks)
    kv_refs = refs[:count]
    refs = refs[count:]
    if not first:
        held_ref, held_tops_ref = refs[:2]
        refs = refs[2:]
    refs = refs[-1:] if last else refs[-2:]
    rows, columns = q_ref.shape
    tok, heads = rows // 2, columns // HD
    lane = lax.broadcasted_iota(jnp.int32, (tok, columns), 1)
    for qv in range(2):
        mine = slice(qv * tok, (qv + 1) * tok)
        q = q_ref[mine]
        apart = jnp.concatenate([jnp.where(lane // HD == h, q, jnp.zeros_like(q)) for h in range(heads)], axis=0)
        scores, biases, values = [], [], []
        for (slot, part, both), kv_ref in zip(blocks, kv_refs):
            base = part * (rows + columns)
            for kvw in (0, 1) if both else (qv,):
                span = slice(kvw * tok, (kvw + 1) * tok)
                keys = kv_ref[base + kvw * tok : base + (kvw + 1) * tok]
                scores.append(lax.dot_general(keys, apart, NT, preferred_element_type=jnp.float32))
                row = BIASES * qv + 2 * slot + kvw
                biases.append(jnp.concatenate([bias_ref[row : row + 1]] * heads, axis=1))
                values.append(kv_ref[base + rows : base + rows + columns, span])
        top = functools.reduce(jnp.maximum, [jnp.max(s, axis=0, keepdims=True) + b for s, b in zip(scores, biases)])
        if not first:
            old_top, old_total = held_tops_ref[2 * qv : 2 * qv + 1], held_tops_ref[2 * qv + 1 : 2 * qv + 2]
            top = jnp.maximum(top, old_top)
            scale = jnp.exp2(old_top - top)
        weights = [jnp.exp2(s - (top - b)) for s, b in zip(scores, biases)]
        total = jnp.sum(functools.reduce(jnp.add, weights), axis=0, keepdims=True)
        if not first:
            total = total + scale * old_total
        rounded = jnp.concatenate([w.astype(jnp.bfloat16) for w in weights], axis=0)
        values = jnp.concatenate(values, axis=1)
        finished = []
        for p in range(heads // 2):
            two = dot(values[2 * p * HD : 2 * (p + 1) * HD], rounded[:, 2 * p * tok : 2 * (p + 1) * tok])
            for h in (2 * p, 2 * p + 1):
                lanes = slice(h * tok, (h + 1) * tok)
                blended = two[(h - 2 * p) * HD : (h - 2 * p + 1) * HD, (h - 2 * p) * tok : (h - 2 * p + 1) * tok]
                at = slice((qv * heads + h) * HD, (qv * heads + h + 1) * HD)
                if not first:
                    blended = blended + scale[:, lanes] * held_ref[at]
                if last:
                    finished.append(blended / total[:, lanes])
                else:
                    refs[0][at] = blended
        if last:
            refs[0][mine] = jnp.concatenate(finished, axis=0).T.astype(jnp.bfloat16)
        else:
            refs[1][2 * qv : 2 * qv + 1] = top
            refs[1][2 * qv + 1 : 2 * qv + 2] = total


def attend(blocks, first, last, bias, q, kvs, state=(), *after):
    rows, columns = q.shape
    tok, heads = rows // 2, columns // HD
    if last:
        out = held((rows, columns), jnp.bfloat16)
    else:
        out = (
            held((2 * columns, tok), jnp.float32),
            held((4, heads * tok), jnp.float32),
        )
    return pl.pallas_call(
        functools.partial(attend_kernel, blocks, first, last),
        out_shape=out,
        in_specs=[VMEM] * (2 + len(kvs) + len(state)) + [ANY] * len(after),
        out_specs=VMEM if last else (VMEM, VMEM),
        compiler_params=params(16),
        cost_estimate=COST,
        name="attend",
    )(bias, q, *kvs, *state, *after)


def pick_kernel(own_ref, a_ref, b_ref, *refs):
    rows = own_ref.shape[0]
    out_ref = refs[-1]
    out_ref[:rows] = own_ref[...]
    first = lax.axis_index("view") & 1 == 0

    @pl.when(first)
    def _():
        out_ref[rows:] = a_ref[...]

    @pl.when(jnp.logical_not(first))
    def _():
        out_ref[rows:] = b_ref[...]


def pick(own, a, b, *after):
    return pl.pallas_call(
        pick_kernel,
        out_shape=held((2 * own.shape[0], own.shape[1]), a.dtype),
        in_specs=[VMEM] * 3 + [ANY] * len(after),
        out_specs=VMEM,
        compiler_params=params(2),
        cost_estimate=COST,
        name="pick",
    )(own, a, b, *after)


def halves_kernel(a_ref, b_ref, after_ref, out_ref):
    half = a_ref.shape[0] // 2
    block = out_ref.shape[1]
    rows = pl.ds(pl.multiple_of((lax.axis_index("view") & 1) * half, half), half)
    for j in range(a_ref.shape[1] // block):
        columns = slice(j * block, (j + 1) * block)
        out_ref[2 * j * half : (2 * j + 1) * half] = a_ref[rows, columns]
        out_ref[(2 * j + 1) * half : (2 * j + 2) * half] = b_ref[rows, columns]


def halves(a, b, after):
    rows, columns = a.shape
    return pl.pallas_call(
        halves_kernel,
        out_shape=held((columns, rows), a.dtype),
        in_specs=[VMEM, VMEM, ANY],
        out_specs=VMEM,
        compiler_params=params(2),
        cost_estimate=COST,
        name="halves",
    )(a, b, after)


def kept_until_kernel(a_ref, after_ref, out_ref):
    out_ref[...] = a_ref[...]


def kept_until(a, after):
    return pl.pallas_call(
        kept_until_kernel,
        out_shape=held(a.shape, a.dtype),
        in_specs=[VMEM, ANY],
        out_specs=VMEM,
        compiler_params=params(2),
        cost_estimate=COST,
        name="kept_until",
    )(a, after)


def feed_kernel(x_ref, a0, a1, a2, a3, o0, o1, mine, pair, win_ref, wback_ref, own_ref, r1, r2, r3):
    head = lax.axis_index("head")
    rows, width = x_ref.shape
    tok = rows // 2
    part = tok // 4

    def turned(ref, columns=slice(None)):
        pieces = []
        for j in range(4):
            for view in range(2):
                start = pl.multiple_of(view * tok + jnp.bitwise_xor(head, j) * part, part)
                pieces.append(ref[pl.ds(start, part), columns])
        return jnp.concatenate(pieces, axis=0)

    block = o0.shape[0]
    core = lax.axis_index("view") & 1
    attention = dot(turned(a0), o0[...]) + dot(turned(a1), o1[...])
    parts = []
    for ref, first, which in ((mine, 0, core), (pair, pair.shape[0] - width, 1 - core)):
        columns = pl.ds(pl.multiple_of(which * (block // 2), block // 2), block // 2)
        both = jnp.concatenate([turned(a3, columns), turned(a2, columns)], axis=1)
        parts.append([dot(both, ref[first + i : first + i + block]) for i in range(0, width, block)])
    attention = attention + jnp.concatenate([m + p for m, p in zip(*parts)], axis=1)
    y = turned(x_ref).astype(jnp.float32) + attention
    normed = (y * lax.rsqrt(jnp.mean(y * y, axis=-1, keepdims=True) + 1e-06)).astype(jnp.bfloat16)
    hidden = jax.nn.gelu(dot(normed, win_ref[...])).astype(jnp.bfloat16)
    update = dot(hidden, wback_ref[...])
    own_ref[...] = attention[: 2 * part] + update[: 2 * part]
    for j, ref in ((1, r1), (2, r2), (3, r3)):
        ref[...] = update[2 * part * j : 2 * part * (j + 1)].astype(jnp.bfloat16)


def feed(x, attended, w_outs, w_in, w_back):
    rows, width = x.shape
    piece = held((rows // 4, width), jnp.bfloat16)
    return pl.pallas_call(
        feed_kernel,
        out_shape=(held((rows // 4, width), jnp.float32), piece, piece, piece),
        in_specs=[VMEM] * 11,
        out_specs=(VMEM,) * 4,
        compiler_params=params(16),
        cost_estimate=COST,
        name="feed",
    )(x, *attended, *w_outs, w_in, w_back)


def gather_kernel(own_ref, r1, r2, r3, kept_ref, sent_ref):
    branch = lax.axis_index("branch")
    part = own_ref.shape[0] // 2
    half = part // 2
    for view in range(2):
        for side, ref in ((1 - branch, sent_ref), (branch, kept_ref)):
            rows = pl.ds(pl.multiple_of(view * part + side * half, half), half)
            total = own_ref[rows, :]
            for r in (r1, r2, r3):
                total = total + r[rows, :].astype(jnp.float32)
            ref[view * half : (view + 1) * half, :] = total.astype(ref.dtype)


def gather(own, received):
    rows, width = own.shape
    return pl.pallas_call(
        gather_kernel,
        out_shape=(
            held((rows // 2, width), jnp.float32),
            held((rows // 2, width), jnp.bfloat16),
        ),
        in_specs=[VMEM] * 4,
        out_specs=(VMEM, VMEM),
        compiler_params=params(2),
        cost_estimate=COST,
        name="gather",
    )(own, *received)


def guide_kernel(guidance_ref, kept_ref, other_ref, out_ref):
    strength = guidance_ref[0]
    weight = jnp.where(lax.axis_index("branch") == 0, strength, 1.0 - strength)
    kept = kept_ref[...]
    guided = weight * kept + (1.0 - weight) * other_ref[...].astype(jnp.float32)
    out_ref[...] = guided.astype(out_ref.dtype)


def guide(guidance, kept, other):
    return pl.pallas_call(
        guide_kernel,
        out_shape=jax.ShapeDtypeStruct(other.shape, jnp.bfloat16),
        in_specs=[SMEM, VMEM, VMEM],
        out_specs=VMEM,
        compiler_params=params(2),
        cost_estimate=COST,
        name="guide",
    )(guidance, kept, other)


def on_device(tokens, partners, counts, w_query, w_key, w_value, w_out, w_in, w_back, guidance):
    per_device, tok, width = tokens.shape[1:]
    x = tokens[0].reshape(per_device * tok, width)
    count = lax.axis_size("view")

    q, kv = project(x, w_query, w_key, w_value)
    bias = biases(count, partners.T, counts)

    near = [shifted("view", count, d)(kv) for d in (2, -2)]
    far = [shifted("view", count, d)(kv) for d in (4, -4)]
    w_1 = flipped("head", 4, 1)(w_out)
    w_01 = halves(w_out, w_1, bias)
    w_32 = flipped("head", 4, 3)(w_01)
    state = attend(((0, 0, True), (2, 0, False), (3, 0, False)), True, False, bias, q, (kv, *near), (), *(w_01,))
    pair = flipped("view", count, 1)(pick(kv, *near, *far, state[1]))
    state = attend(((5, 0, False), (6, 0, False)), False, False, bias, q, far, state, w_32)
    attended = attend(((1, 0, True), (4, 1, True)), False, True, bias, q, (pair, pair), state)
    w_pair = flipped("view", count, 1)(kept_until(w_32, attended))

    pieces = [attended] + [flipped("head", 4, j)(attended) for j in (1, 2, 3)]
    own, *outgoing = feed(x, pieces, (w_out, w_1, w_32, w_pair), w_in, w_back)
    received = [flipped("head", 4, j)(r) for j, r in zip((1, 2, 3), outgoing)]
    kept, sent = gather(own, received)
    other = flipped("branch", 2, 1)(sent)
    return guide(guidance, kept, other).reshape(per_device, -1, width)


def solution(mesh):
    placed = (
        P("branch", "view", None, None),
        P(None, "view"),
        P("view"),
        P(None, "head"),
        P(None, "head"),
        P(None, "head"),
        P("head", None),
        P(None, "head"),
        P("head", None),
        P(),
    )
    return jax.shard_map(
        on_device,
        mesh=mesh,
        in_specs=placed,
        out_specs=P("view", ("head", "branch"), None),
        check_vma=False,
    )
```

```python
import functools

import jax
import jax.numpy as jnp
from jax import lax
from jax.experimental import pallas as pl
from jax.experimental.pallas import tpu as pltpu
from jax.sharding import PartitionSpec as P

HD = 64
ROUNDS = 8
BIASES = 16
DIAGONAL = (2, 3, 5, 6)
MASKED = -1e30
LOG2E = 1.4426950408889634

NT = (((1,), (1,)), ((), ()))
VMEM = pl.BlockSpec(memory_space=pltpu.VMEM)
SMEM = pl.BlockSpec(memory_space=pltpu.SMEM)
HBM = pl.BlockSpec(memory_space=pltpu.HBM)
ANY = pl.BlockSpec(memory_space=pl.ANY)


def params(mib):
    return pltpu.CompilerParams(vmem_limit_bytes=int(mib * 1024 * 1024))


def shifted(axis, count, apart):
    return functools.partial(lax.ppermute, axis_name=axis, perm=[(i, (i - apart) % count) for i in range(count)])


def flipped(axis, count, bits):
    return functools.partial(lax.ppermute, axis_name=axis, perm=[(i, i ^ bits) for i in range(count)])


def held(shape, dtype):
    return pltpu.VMEM(shape, dtype)


def outside(*arrays):
    return tuple(pltpu.with_memory_space_constraint(a, pltpu.HBM) for a in arrays)


COST = pl.CostEstimate(flops=1000, bytes_accessed=1000, transcendentals=0)


def dot(a, b):
    return jnp.dot(a, b, preferred_element_type=jnp.float32)


def chunked(source, target, sems, count):
    rows = source.shape[0] // count
    pieces = [pl.ds(i * rows, rows) for i in range(count)]
    return [pltpu.make_async_copy(source.at[p], target.at[p], sems.at[i]) for i, p in enumerate(pieces)]


def key_views(count):
    me = lax.axis_index("view")
    core = me & 1
    sources = (me, me + 1 - 2 * core, me + 2, me - 2, me - 1 + 2 * core, me + 4, me - 4)
    return [2 * lax.rem(s + count, count) for s in sources]


def bias_kernel(count, partners_ref, counts_ref, after_ref, bias_ref):
    bias_ref[...] = jnp.zeros_like(bias_ref)
    firsts = key_views(count)
    for qv in range(2):
        used = counts_ref[qv]
        named = [jnp.where(r < used, partners_ref[qv, r], -1) for r in range(ROUNDS)]
        for slot, first in enumerate(firsts):
            for kvw in range(2):
                if (slot in DIAGONAL or slot == 0) and (kvw == qv) == (slot == 0):
                    continue
                times = sum((n == first + kvw).astype(jnp.int32) for n in named)
                row = BIASES * qv + 2 * slot + kvw
                bias_ref[row : row + 1] = jnp.full((1, bias_ref.shape[1]), times.astype(jnp.float32))
    times = bias_ref[...]
    bias_ref[...] = jnp.where(times > 0, jnp.log2(jnp.maximum(times, 1.0)), MASKED)
    for qv in range(2):
        row = BIASES * qv + qv
        bias_ref[row : row + 1] = jnp.zeros((1, bias_ref.shape[1]), jnp.float32)


def biases(count, partners, counts, after):
    return pl.pallas_call(
        functools.partial(bias_kernel, count),
        out_shape=held((2 * BIASES, 2 * HD), jnp.float32),
        in_specs=[SMEM, SMEM, ANY],
        out_specs=VMEM,
        compiler_params=params(2),
        cost_estimate=COST,
        name="biases",
    )(partners, counts, after)


def project_kernel(x_hbm, wk_hbm, wv_hbm, wo_hbm, x_ref, kv_ref, half_ref, wk, wv, sems):
    half = half_ref.shape[0]
    mine = pl.ds(pl.multiple_of((lax.axis_index("view") & 1) * half, half), half)
    pairs = ((x_hbm, x_ref), (wk_hbm, wk), (wv_hbm, wv), (wo_hbm.at[mine], half_ref))
    loads = [pltpu.make_async_copy(source, target, sems.at[i]) for i, (source, target) in enumerate(pairs)]
    for copy in loads:
        copy.start()
    rows = x_ref.shape[0]
    loads[0].wait()
    loads[1].wait()
    kv_ref[:rows] = dot(x_ref[...], wk[...]).astype(jnp.bfloat16)
    loads[2].wait()
    kv_ref[rows:] = dot(x_ref[...], wv[...]).T.astype(jnp.bfloat16)
    loads[3].wait()


def project(x, w_key, w_value, w_out):
    rows, width = x.shape
    columns = w_key.shape[1]
    return pl.pallas_call(
        project_kernel,
        out_shape=(
            held(x.shape, x.dtype),
            held((rows + columns, rows), jnp.bfloat16),
            held((w_out.shape[0] // 2, w_out.shape[1]), w_out.dtype),
        ),
        in_specs=[HBM] * 4,
        out_specs=(VMEM,) * 3,
        scratch_shapes=[pltpu.VMEM((width, columns), jnp.bfloat16)] * 2 + [pltpu.SemaphoreType.DMA((4,))],
        compiler_params=params(8),
        cost_estimate=COST,
        name="project",
    )(*outside(x, w_key, w_value, w_out))


def ask_kernel(x_ref, wq_ref, after_ref, q_ref):
    q_ref[...] = (dot(x_ref[...], wq_ref[...]) * (HD ** (-0.5) * LOG2E)).astype(jnp.bfloat16)


def ask(x, w_query, after):
    return pl.pallas_call(
        ask_kernel,
        out_shape=held((x.shape[0], w_query.shape[1]), jnp.bfloat16),
        in_specs=[VMEM, VMEM, ANY],
        out_specs=VMEM,
        compiler_params=params(4),
        cost_estimate=COST,
        name="ask",
    )(x, w_query, after)


def attend_kernel(blocks, first, last, bias_ref, q_ref, *refs):
    count = len(blocks)
    kv_refs = refs[:count]
    refs = refs[count:]
    if not first:
        held_ref, held_tops_ref = refs[:2]
        refs = refs[2:]
    refs = refs[-1:] if last else refs[-2:]
    rows, columns = q_ref.shape
    tok, heads = rows // 2, columns // HD
    lane = lax.broadcasted_iota(jnp.int32, (tok, columns), 1)
    for qv in range(2):
        mine = slice(qv * tok, (qv + 1) * tok)
        q = q_ref[mine]
        apart = jnp.concatenate([jnp.where(lane // HD == h, q, jnp.zeros_like(q)) for h in range(heads)], axis=0)
        scores, biases, values = [], [], []
        for (slot, part, both), kv_ref in zip(blocks, kv_refs):
            base = part * (rows + columns)
            for kvw in (0, 1) if both else (qv,):
                span = slice(kvw * tok, (kvw + 1) * tok)
                keys = kv_ref[base + kvw * tok : base + (kvw + 1) * tok]
                scores.append(lax.dot_general(keys, apart, NT, preferred_element_type=jnp.float32))
                row = BIASES * qv + 2 * slot + kvw
                biases.append(jnp.concatenate([bias_ref[row : row + 1]] * heads, axis=1))
                values.append(kv_ref[base + rows : base + rows + columns, span])
        top = functools.reduce(jnp.maximum, [jnp.max(s, axis=0, keepdims=True) + b for s, b in zip(scores, biases)])
        if not first:
            old_top, old_total = held_tops_ref[2 * qv : 2 * qv + 1], held_tops_ref[2 * qv + 1 : 2 * qv + 2]
            top = jnp.maximum(top, old_top)
            scale = jnp.exp2(old_top - top)
        weights = [jnp.exp2(s - (top - b)) for s, b in zip(scores, biases)]
        total = jnp.sum(functools.reduce(jnp.add, weights), axis=0, keepdims=True)
        if not first:
            total = total + scale * old_total
        rounded = jnp.concatenate([w.astype(jnp.bfloat16) for w in weights], axis=0)
        values = jnp.concatenate(values, axis=1)
        finished = []
        for p in range(heads // 2):
            two = dot(values[2 * p * HD : 2 * (p + 1) * HD], rounded[:, 2 * p * tok : 2 * (p + 1) * tok])
            for h in (2 * p, 2 * p + 1):
                lanes = slice(h * tok, (h + 1) * tok)
                blended = two[(h - 2 * p) * HD : (h - 2 * p + 1) * HD, (h - 2 * p) * tok : (h - 2 * p + 1) * tok]
                at = slice((qv * heads + h) * HD, (qv * heads + h + 1) * HD)
                if not first:
                    blended = blended + scale[:, lanes] * held_ref[at]
                if last:
                    finished.append(blended / total[:, lanes])
                else:
                    refs[0][at] = blended
        if last:
            refs[0][mine] = jnp.concatenate(finished, axis=0).T.astype(jnp.bfloat16)
        else:
            refs[1][2 * qv : 2 * qv + 1] = top
            refs[1][2 * qv + 1 : 2 * qv + 2] = total


def attend(blocks, first, last, bias, q, kvs, state=(), *after):
    rows, columns = q.shape
    tok, heads = rows // 2, columns // HD
    if last:
        out = held((rows, columns), jnp.bfloat16)
    else:
        out = (
            held((2 * columns, tok), jnp.float32),
            held((4, heads * tok), jnp.float32),
        )
    return pl.pallas_call(
        functools.partial(attend_kernel, blocks, first, last),
        out_shape=out,
        in_specs=[VMEM] * (2 + len(kvs) + len(state)) + [ANY] * len(after),
        out_specs=VMEM if last else (VMEM, VMEM),
        compiler_params=params(16),
        cost_estimate=COST,
        name="attend",
    )(bias, q, *kvs, *state, *after)


def pick_kernel(a_ref, b_ref, *refs):
    out_ref = refs[-1]
    first = lax.axis_index("view") & 1 == 0

    @pl.when(first)
    def _():
        out_ref[...] = a_ref[...]

    @pl.when(jnp.logical_not(first))
    def _():
        out_ref[...] = b_ref[...]


def pick(a, b, *after):
    return pl.pallas_call(
        pick_kernel,
        out_shape=held(a.shape, a.dtype),
        in_specs=[VMEM] * 2 + [ANY] * len(after),
        out_specs=VMEM,
        compiler_params=params(2),
        cost_estimate=COST,
        name="pick",
    )(a, b, *after)


def halves_kernel(a_ref, b_ref, out_ref):
    half = a_ref.shape[0]
    block = out_ref.shape[1]
    rows = pl.ds(pl.multiple_of((lax.axis_index("view") & 1) * half, half), half)
    for j in range(a_ref.shape[1] // block):
        columns = slice(j * block, (j + 1) * block)
        out_ref[2 * j * half : (2 * j + 1) * half] = a_ref[:, columns]
        out_ref[(2 * j + 1) * half : (2 * j + 2) * half] = b_ref[rows, columns]


def halves(a, b):
    rows, columns = b.shape
    return pl.pallas_call(
        halves_kernel,
        out_shape=held((columns, rows), a.dtype),
        in_specs=[VMEM, VMEM],
        out_specs=VMEM,
        compiler_params=params(2),
        cost_estimate=COST,
        name="halves",
    )(a, b)


def kept_until_kernel(a_ref, after_ref, out_ref):
    out_ref[...] = a_ref[...]


def kept_until(a, after):
    return pl.pallas_call(
        kept_until_kernel,
        out_shape=held(a.shape, a.dtype),
        in_specs=[VMEM, ANY],
        out_specs=VMEM,
        compiler_params=params(2),
        cost_estimate=COST,
        name="kept_until",
    )(a, after)


def feed_kernel(x_ref, a0, a1, a2, a3, o0, o1, mine, pair, win_ref, wback_ref, own_ref, r1, r2, r3):
    head = lax.axis_index("head")
    rows, width = x_ref.shape
    tok = rows // 2
    part = tok // 4

    def turned(ref, columns=slice(None)):
        pieces = []
        for j in range(4):
            for view in range(2):
                start = pl.multiple_of(view * tok + jnp.bitwise_xor(head, j) * part, part)
                pieces.append(ref[pl.ds(start, part), columns])
        return jnp.concatenate(pieces, axis=0)

    block = o0.shape[0]
    core = lax.axis_index("view") & 1
    attention = dot(turned(a0), o0[...]) + dot(turned(a1), o1[...])
    parts = []
    for ref, first, which in ((mine, 0, core), (pair, pair.shape[0] - width, 1 - core)):
        columns = pl.ds(pl.multiple_of(which * (block // 2), block // 2), block // 2)
        both = jnp.concatenate([turned(a3, columns), turned(a2, columns)], axis=1)
        parts.append([dot(both, ref[first + i : first + i + block]) for i in range(0, width, block)])
    attention = attention + jnp.concatenate([m + p for m, p in zip(*parts)], axis=1)
    y = turned(x_ref).astype(jnp.float32) + attention
    normed = (y * lax.rsqrt(jnp.mean(y * y, axis=-1, keepdims=True) + 1e-06)).astype(jnp.bfloat16)
    hidden = jax.nn.gelu(dot(normed, win_ref[...])).astype(jnp.bfloat16)
    update = dot(hidden, wback_ref[...])
    own_ref[...] = attention[: 2 * part] + update[: 2 * part]
    for j, ref in ((1, r1), (2, r2), (3, r3)):
        ref[...] = update[2 * part * j : 2 * part * (j + 1)].astype(jnp.bfloat16)


def feed(x, attended, w_outs, w_in, w_back):
    rows, width = x.shape
    piece = held((rows // 4, width), jnp.bfloat16)
    return pl.pallas_call(
        feed_kernel,
        out_shape=(held((rows // 4, width), jnp.float32), piece, piece, piece),
        in_specs=[VMEM] * 11,
        out_specs=(VMEM,) * 4,
        compiler_params=params(16),
        cost_estimate=COST,
        name="feed",
    )(x, *attended, *w_outs, w_in, w_back)


def gather_kernel(own_ref, r1, r2, r3, kept_ref, sent_ref):
    branch = lax.axis_index("branch")
    part = own_ref.shape[0] // 2
    half = part // 2
    for view in range(2):
        for side, ref in ((1 - branch, sent_ref), (branch, kept_ref)):
            rows = pl.ds(pl.multiple_of(view * part + side * half, half), half)
            total = own_ref[rows, :]
            for r in (r1, r2, r3):
                total = total + r[rows, :].astype(jnp.float32)
            ref[view * half : (view + 1) * half, :] = total.astype(ref.dtype)


def gather(own, received):
    rows, width = own.shape
    return pl.pallas_call(
        gather_kernel,
        out_shape=(
            held((rows // 2, width), jnp.float32),
            held((rows // 2, width), jnp.bfloat16),
        ),
        in_specs=[VMEM] * 4,
        out_specs=(VMEM, VMEM),
        compiler_params=params(2),
        cost_estimate=COST,
        name="gather",
    )(own, *received)


def guide_kernel(guidance_ref, kept_ref, other_ref, out_ref):
    strength = guidance_ref[0]
    weight = jnp.where(lax.axis_index("branch") == 0, strength, 1.0 - strength)
    kept = kept_ref[...]
    guided = weight * kept + (1.0 - weight) * other_ref[...].astype(jnp.float32)
    out_ref[...] = guided.astype(out_ref.dtype)


def guide(guidance, kept, other):
    return pl.pallas_call(
        guide_kernel,
        out_shape=jax.ShapeDtypeStruct(other.shape, jnp.bfloat16),
        in_specs=[SMEM, VMEM, VMEM],
        out_specs=VMEM,
        compiler_params=params(2),
        cost_estimate=COST,
        name="guide",
    )(guidance, kept, other)


def on_device(tokens, partners, counts, w_query, w_key, w_value, w_out, w_in, w_back, guidance):
    per_device, tok, width = tokens.shape[1:]
    x = tokens[0].reshape(per_device * tok, width)
    count = lax.axis_size("view")

    x, kv, w_half = project(x, w_key, w_value, w_out)

    near = [shifted("view", count, d)(kv) for d in (2, -2)]
    far = [shifted("view", count, d)(kv) for d in (4, -4)]
    w_1 = flipped("head", 4, 1)(w_out)
    w_01 = halves(w_half, w_1)
    q = ask(x, w_query, w_01)
    bias = biases(count, partners.T, counts, w_01)
    w_32 = flipped("head", 4, 3)(w_01)
    state = attend(((0, 0, True), (2, 0, False), (3, 0, False)), True, False, bias, q, (kv, *near), (), *(w_01,))
    other_core = flipped("view", count, 1)
    other, cross = other_core(kv), other_core(pick(*near, *far, state[1]))
    state = attend(((1, 0, True), (5, 0, False), (6, 0, False)), False, False, bias, q, (other, *far), state)
    attended = attend(((4, 0, True),), False, True, bias, q, (cross,), state, w_32)
    w_pair = flipped("view", count, 1)(kept_until(w_32, attended))

    pieces = [attended] + [flipped("head", 4, j)(attended) for j in (1, 2, 3)]
    own, *outgoing = feed(x, pieces, (w_out, w_1, w_32, w_pair), w_in, w_back)
    received = [flipped("head", 4, j)(r) for j, r in zip((1, 2, 3), outgoing)]
    kept, sent = gather(own, received)
    other = flipped("branch", 2, 1)(sent)
    return guide(guidance, kept, other).reshape(per_device, -1, width)


def solution(mesh):
    placed = (
        P("branch", "view", None, None),
        P(None, "view"),
        P("view"),
        P(None, "head"),
        P(None, "head"),
        P(None, "head"),
        P("head", None),
        P(None, "head"),
        P("head", None),
        P(),
    )
    return jax.shard_map(
        on_device,
        mesh=mesh,
        in_specs=placed,
        out_specs=P("view", ("head", "branch"), None),
        check_vma=False,
    )
```

```python
import functools

import jax
import jax.numpy as jnp
from jax import lax
from jax.experimental import pallas as pl
from jax.experimental.pallas import tpu as pltpu
from jax.sharding import PartitionSpec as P

HD = 64
ROUNDS = 8
BIASES = 16
DIAGONAL = (2, 3, 5, 6)
MASKED = -1e30
LOG2E = 1.4426950408889634

NT = (((1,), (1,)), ((), ()))
VMEM = pl.BlockSpec(memory_space=pltpu.VMEM)
SMEM = pl.BlockSpec(memory_space=pltpu.SMEM)
HBM = pl.BlockSpec(memory_space=pltpu.HBM)
ANY = pl.BlockSpec(memory_space=pl.ANY)


def params(mib):
    return pltpu.CompilerParams(vmem_limit_bytes=int(mib * 1024 * 1024))


def matched(count, apart, parity):
    route = []
    for low in range(count):
        if (low // apart) % 2 == parity:
            high = (low + apart) % count
            route += [(low, high), (high, low)]
    return functools.partial(lax.ppermute, axis_name="view", perm=route)


def onward(count):
    route = [(i, (i + 8 - 4 * (i & 4)) % count) for i in range(count)]
    return functools.partial(lax.ppermute, axis_name="view", perm=route)


def flipped(axis, count, bits):
    return functools.partial(lax.ppermute, axis_name=axis, perm=[(i, i ^ bits) for i in range(count)])


def held(shape, dtype):
    return pltpu.VMEM(shape, dtype)


def outside(*arrays):
    return tuple(pltpu.with_memory_space_constraint(a, pltpu.HBM) for a in arrays)


COST = pl.CostEstimate(flops=1000, bytes_accessed=1000, transcendentals=0)


def dot(a, b):
    return jnp.dot(a, b, preferred_element_type=jnp.float32)


def chunked(source, target, sems, count):
    rows = source.shape[0] // count
    pieces = [pl.ds(i * rows, rows) for i in range(count)]
    return [pltpu.make_async_copy(source.at[p], target.at[p], sems.at[i]) for i, p in enumerate(pieces)]


def key_views(count):
    me = lax.axis_index("view")
    core = me & 1
    near, far = 2 * (me & 2) - 2, 4 - 2 * (me & 4)
    sources = (me, me + 1 - 2 * core, me + near, me - near, me - 1 + 2 * core, me + far, me - far)
    return [2 * lax.rem(s + count, count) for s in sources]


def bias_kernel(count, partners_ref, counts_ref, after_ref, bias_ref):
    bias_ref[...] = jnp.zeros_like(bias_ref)
    firsts = key_views(count)
    for qv in range(2):
        used = counts_ref[qv]
        named = [jnp.where(r < used, partners_ref[qv, r], -1) for r in range(ROUNDS)]
        for slot, first in enumerate(firsts):
            for kvw in range(2):
                if (slot in DIAGONAL or slot == 0) and (kvw == qv) == (slot == 0):
                    continue
                times = sum((n == first + kvw).astype(jnp.int32) for n in named)
                row = BIASES * qv + 2 * slot + kvw
                bias_ref[row : row + 1] = jnp.full((1, bias_ref.shape[1]), times.astype(jnp.float32))
    times = bias_ref[...]
    bias_ref[...] = jnp.where(times > 0, jnp.log2(jnp.maximum(times, 1.0)), MASKED)
    for qv in range(2):
        row = BIASES * qv + qv
        bias_ref[row : row + 1] = jnp.zeros((1, bias_ref.shape[1]), jnp.float32)


def biases(count, partners, counts, after):
    return pl.pallas_call(
        functools.partial(bias_kernel, count),
        out_shape=held((2 * BIASES, 2 * HD), jnp.float32),
        in_specs=[SMEM, SMEM, ANY],
        out_specs=VMEM,
        compiler_params=params(2),
        cost_estimate=COST,
        name="biases",
    )(partners, counts, after)


def project_kernel(x_hbm, wk_hbm, wv_hbm, wo_hbm, x_ref, kv_ref, half_ref, wk, wv, sems):
    half = half_ref.shape[0]
    mine = pl.ds(pl.multiple_of((lax.axis_index("view") & 1) * half, half), half)
    pairs = ((x_hbm, x_ref), (wk_hbm, wk), (wv_hbm, wv), (wo_hbm.at[mine], half_ref))
    loads = [pltpu.make_async_copy(source, target, sems.at[i]) for i, (source, target) in enumerate(pairs)]
    for copy in loads:
        copy.start()
    rows = x_ref.shape[0]
    loads[0].wait()
    loads[1].wait()
    kv_ref[:rows] = dot(x_ref[...], wk[...]).astype(jnp.bfloat16)
    loads[2].wait()
    kv_ref[rows:] = dot(x_ref[...], wv[...]).T.astype(jnp.bfloat16)
    loads[3].wait()


def project(x, w_key, w_value, w_out):
    rows, width = x.shape
    columns = w_key.shape[1]
    return pl.pallas_call(
        project_kernel,
        out_shape=(
            held(x.shape, x.dtype),
            held((rows + columns, rows), jnp.bfloat16),
            held((w_out.shape[0] // 2, w_out.shape[1]), w_out.dtype),
        ),
        in_specs=[HBM] * 4,
        out_specs=(VMEM,) * 3,
        scratch_shapes=[pltpu.VMEM((width, columns), jnp.bfloat16)] * 2 + [pltpu.SemaphoreType.DMA((4,))],
        compiler_params=params(8),
        cost_estimate=COST,
        name="project",
    )(*outside(x, w_key, w_value, w_out))


def ask_kernel(x_ref, wq_ref, after_ref, q_ref):
    q_ref[...] = (dot(x_ref[...], wq_ref[...]) * (HD ** (-0.5) * LOG2E)).astype(jnp.bfloat16)


def ask(x, w_query, after):
    return pl.pallas_call(
        ask_kernel,
        out_shape=held((x.shape[0], w_query.shape[1]), jnp.bfloat16),
        in_specs=[VMEM, VMEM, ANY],
        out_specs=VMEM,
        compiler_params=params(4),
        cost_estimate=COST,
        name="ask",
    )(x, w_query, after)


def attend_kernel(blocks, first, last, bias_ref, q_ref, *refs):
    count = len(blocks)
    kv_refs = refs[:count]
    refs = refs[count:]
    if not first:
        held_ref, held_tops_ref = refs[:2]
        refs = refs[2:]
    refs = refs[-1:] if last else refs[-2:]
    rows, columns = q_ref.shape
    tok, heads = rows // 2, columns // HD
    lane = lax.broadcasted_iota(jnp.int32, (tok, columns), 1)
    for qv in range(2):
        mine = slice(qv * tok, (qv + 1) * tok)
        q = q_ref[mine]
        apart = jnp.concatenate([jnp.where(lane // HD == h, q, jnp.zeros_like(q)) for h in range(heads)], axis=0)
        scores, biases, values = [], [], []
        for (slot, part, both), kv_ref in zip(blocks, kv_refs):
            base = part * (rows + columns)
            for kvw in (0, 1) if both else (qv,):
                span = slice(kvw * tok, (kvw + 1) * tok)
                keys = kv_ref[base + kvw * tok : base + (kvw + 1) * tok]
                scores.append(lax.dot_general(keys, apart, NT, preferred_element_type=jnp.float32))
                row = BIASES * qv + 2 * slot + kvw
                biases.append(jnp.concatenate([bias_ref[row : row + 1]] * heads, axis=1))
                values.append(kv_ref[base + rows : base + rows + columns, span])
        top = functools.reduce(jnp.maximum, [jnp.max(s, axis=0, keepdims=True) + b for s, b in zip(scores, biases)])
        if not first:
            old_top, old_total = held_tops_ref[2 * qv : 2 * qv + 1], held_tops_ref[2 * qv + 1 : 2 * qv + 2]
            top = jnp.maximum(top, old_top)
            scale = jnp.exp2(old_top - top)
        weights = [jnp.exp2(s - (top - b)) for s, b in zip(scores, biases)]
        total = jnp.sum(functools.reduce(jnp.add, weights), axis=0, keepdims=True)
        if not first:
            total = total + scale * old_total
        rounded = jnp.concatenate([w.astype(jnp.bfloat16) for w in weights], axis=0)
        values = jnp.concatenate(values, axis=1)
        finished = []
        for p in range(heads // 2):
            two = dot(values[2 * p * HD : 2 * (p + 1) * HD], rounded[:, 2 * p * tok : 2 * (p + 1) * tok])
            for h in (2 * p, 2 * p + 1):
                lanes = slice(h * tok, (h + 1) * tok)
                blended = two[(h - 2 * p) * HD : (h - 2 * p + 1) * HD, (h - 2 * p) * tok : (h - 2 * p + 1) * tok]
                at = slice((qv * heads + h) * HD, (qv * heads + h + 1) * HD)
                if not first:
                    blended = blended + scale[:, lanes] * held_ref[at]
                if last:
                    finished.append(blended / total[:, lanes])
                else:
                    refs[0][at] = blended
        if last:
            refs[0][mine] = jnp.concatenate(finished, axis=0).T.astype(jnp.bfloat16)
        else:
            refs[1][2 * qv : 2 * qv + 1] = top
            refs[1][2 * qv + 1 : 2 * qv + 2] = total


def attend(blocks, first, last, bias, q, kvs, state=(), *after):
    rows, columns = q.shape
    tok, heads = rows // 2, columns // HD
    if last:
        out = held((rows, columns), jnp.bfloat16)
    else:
        out = (
            held((2 * columns, tok), jnp.float32),
            held((4, heads * tok), jnp.float32),
        )
    return pl.pallas_call(
        functools.partial(attend_kernel, blocks, first, last),
        out_shape=out,
        in_specs=[VMEM] * (2 + len(kvs) + len(state)) + [ANY] * len(after),
        out_specs=VMEM if last else (VMEM, VMEM),
        compiler_params=params(16),
        cost_estimate=COST,
        name="attend",
    )(bias, q, *kvs, *state, *after)


def pick_kernel(a_ref, b_ref, *refs):
    out_ref = refs[-1]
    me = lax.axis_index("view")
    first = (me & 1) != ((me >> 1) & 1)

    @pl.when(first)
    def _():
        out_ref[...] = a_ref[...]

    @pl.when(jnp.logical_not(first))
    def _():
        out_ref[...] = b_ref[...]


def pick(a, b, *after):
    return pl.pallas_call(
        pick_kernel,
        out_shape=held(a.shape, a.dtype),
        in_specs=[VMEM] * 2 + [ANY] * len(after),
        out_specs=VMEM,
        compiler_params=params(2),
        cost_estimate=COST,
        name="pick",
    )(a, b, *after)


def stack_kernel(*refs):
    *piece_refs, _, out_ref = refs
    at = 0
    for ref in piece_refs:
        out_ref[at : at + ref.shape[0]] = ref[...]
        at += ref.shape[0]


def stack(*pieces, after):
    return pl.pallas_call(
        stack_kernel,
        out_shape=held((sum(p.shape[0] for p in pieces), pieces[0].shape[1]), pieces[0].dtype),
        in_specs=[VMEM] * len(pieces) + [ANY],
        out_specs=VMEM,
        compiler_params=params(2),
        cost_estimate=COST,
        name="stack",
    )(*pieces, after)


def feed_kernel(x_ref, a0, a1, a2, a3, o0, w1, w32, pair, win_ref, wback_ref, own_ref, r1, r2, r3):
    head = lax.axis_index("head")
    rows, width = x_ref.shape
    tok = rows // 2
    part = tok // 4

    def turned(ref, columns=slice(None)):
        pieces = []
        for j in range(4):
            for view in range(2):
                start = pl.multiple_of(view * tok + jnp.bitwise_xor(head, j) * part, part)
                pieces.append(ref[pl.ds(start, part), columns])
        return jnp.concatenate(pieces, axis=0)

    half = w1.shape[0]
    core = lax.axis_index("view") & 1
    mine = pl.ds(pl.multiple_of(core * half, half), half)
    theirs = pl.ds(pl.multiple_of((1 - core) * half, half), half)
    left = jnp.concatenate([turned(a, rows) for a in (a1, a3, a2) for rows in (mine, theirs)], axis=1)
    own = (w1[...], w32[:half], w32[half:])
    right = [r for i, w in enumerate(own) for r in (w, pair[i * half : (i + 1) * half])]
    attention = dot(turned(a0), o0[...]) + dot(left, jnp.concatenate(right, axis=0))
    y = turned(x_ref).astype(jnp.float32) + attention
    normed = (y * lax.rsqrt(jnp.mean(y * y, axis=-1, keepdims=True) + 1e-06)).astype(jnp.bfloat16)
    hidden = jax.nn.gelu(dot(normed, win_ref[...])).astype(jnp.bfloat16)
    update = dot(hidden, wback_ref[...])
    own_ref[...] = attention[: 2 * part] + update[: 2 * part]
    for j, ref in ((1, r1), (2, r2), (3, r3)):
        ref[...] = update[2 * part * j : 2 * part * (j + 1)].astype(jnp.bfloat16)


def feed(x, attended, w_outs, w_in, w_back):
    rows, width = x.shape
    piece = held((rows // 4, width), jnp.bfloat16)
    return pl.pallas_call(
        feed_kernel,
        out_shape=(held((rows // 4, width), jnp.float32), piece, piece, piece),
        in_specs=[VMEM] * 11,
        out_specs=(VMEM,) * 4,
        compiler_params=params(16),
        cost_estimate=COST,
        name="feed",
    )(x, *attended, *w_outs, w_in, w_back)


def gather_kernel(own_ref, r1, r2, r3, kept_ref, sent_ref):
    branch = lax.axis_index("branch")
    part = own_ref.shape[0] // 2
    half = part // 2
    for view in range(2):
        for side, ref in ((1 - branch, sent_ref), (branch, kept_ref)):
            rows = pl.ds(pl.multiple_of(view * part + side * half, half), half)
            total = own_ref[rows, :]
            for r in (r1, r2, r3):
                total = total + r[rows, :].astype(jnp.float32)
            ref[view * half : (view + 1) * half, :] = total.astype(ref.dtype)


def gather(own, received):
    rows, width = own.shape
    return pl.pallas_call(
        gather_kernel,
        out_shape=(
            held((rows // 2, width), jnp.float32),
            held((rows // 2, width), jnp.bfloat16),
        ),
        in_specs=[VMEM] * 4,
        out_specs=(VMEM, VMEM),
        compiler_params=params(2),
        cost_estimate=COST,
        name="gather",
    )(own, *received)


def guide_kernel(guidance_ref, kept_ref, other_ref, out_ref):
    strength = guidance_ref[0]
    weight = jnp.where(lax.axis_index("branch") == 0, strength, 1.0 - strength)
    kept = kept_ref[...]
    guided = weight * kept + (1.0 - weight) * other_ref[...].astype(jnp.float32)
    out_ref[...] = guided.astype(out_ref.dtype)


def guide(guidance, kept, other):
    return pl.pallas_call(
        guide_kernel,
        out_shape=jax.ShapeDtypeStruct(other.shape, jnp.bfloat16),
        in_specs=[SMEM, VMEM, VMEM],
        out_specs=VMEM,
        compiler_params=params(2),
        cost_estimate=COST,
        name="guide",
    )(guidance, kept, other)


def on_device(tokens, partners, counts, w_query, w_key, w_value, w_out, w_in, w_back, guidance):
    per_device, tok, width = tokens.shape[1:]
    x = tokens[0].reshape(per_device * tok, width)
    count = lax.axis_size("view")

    x, kv, w_half = project(x, w_key, w_value, w_out)

    near = [matched(count, 2, parity)(kv) for parity in (1, 0)]
    across = flipped("view", count, 4)(kv)
    far = (across, onward(count)(across))
    w_1 = flipped("head", 4, 1)(w_half)
    w_32 = flipped("head", 4, 3)(stack(w_half, w_1, after=x))
    q = ask(x, w_query, x)
    bias = biases(count, partners.T, counts, x)
    state = attend(((0, 0, True), (2, 0, False), (3, 0, False)), True, False, bias, q, (kv, *near))
    other_core = flipped("view", count, 1)
    other, cross = other_core(kv), other_core(pick(*near, *far, state[1]))
    state = attend(((1, 0, True), (5, 0, False), (6, 0, False)), False, False, bias, q, (other, *far), state, w_32)
    attended = attend(((4, 0, True),), False, True, bias, q, (cross,), state)
    w_pair = other_core(stack(w_1, w_32, after=attended))

    pieces = [attended] + [flipped("head", 4, j)(attended) for j in (1, 2, 3)]
    own, *outgoing = feed(x, pieces, (w_out, w_1, w_32, w_pair), w_in, w_back)
    received = [flipped("head", 4, j)(r) for j, r in zip((1, 2, 3), outgoing)]
    kept, sent = gather(own, received)
    other = flipped("branch", 2, 1)(sent)
    return guide(guidance, kept, other).reshape(per_device, -1, width)


def solution(mesh):
    placed = (
        P("branch", "view", None, None),
        P(None, "view"),
        P("view"),
        P(None, "head"),
        P(None, "head"),
        P(None, "head"),
        P("head", None),
        P(None, "head"),
        P("head", None),
        P(),
    )
    return jax.shard_map(
        on_device,
        mesh=mesh,
        in_specs=placed,
        out_specs=P("view", ("head", "branch"), None),
        check_vma=False,
    )
```

```python
import functools

import jax
import jax.numpy as jnp
from jax import lax
from jax.experimental import pallas as pl
from jax.experimental.pallas import tpu as pltpu
from jax.sharding import PartitionSpec as P

HD = 64
ROUNDS = 8
BIASES = 16
DIAGONAL = (2, 3, 5, 6)
MASKED = -1e30
LOG2E = 1.4426950408889634

NT = (((1,), (1,)), ((), ()))
VMEM = pl.BlockSpec(memory_space=pltpu.VMEM)
SMEM = pl.BlockSpec(memory_space=pltpu.SMEM)
HBM = pl.BlockSpec(memory_space=pltpu.HBM)
ANY = pl.BlockSpec(memory_space=pl.ANY)


def params(mib):
    return pltpu.CompilerParams(vmem_limit_bytes=int(mib * 1024 * 1024))


def matched(count, apart, parity):
    route = []
    for low in range(count):
        if (low // apart) % 2 == parity:
            high = (low + apart) % count
            route += [(low, high), (high, low)]
    return functools.partial(lax.ppermute, axis_name="view", perm=route)


def onward(count):
    route = [(i, (i + 8 - 4 * (i & 4)) % count) for i in range(count)]
    return functools.partial(lax.ppermute, axis_name="view", perm=route)


def flipped(axis, count, bits):
    return functools.partial(lax.ppermute, axis_name=axis, perm=[(i, i ^ bits) for i in range(count)])


def held(shape, dtype):
    return pltpu.VMEM(shape, dtype)


def outside(*arrays):
    return tuple(pltpu.with_memory_space_constraint(a, pltpu.HBM) for a in arrays)


COST = pl.CostEstimate(flops=1000, bytes_accessed=1000, transcendentals=0)


def dot(a, b):
    return jnp.dot(a, b, preferred_element_type=jnp.float32)


def chunked(source, target, sems, count):
    rows = source.shape[0] // count
    pieces = [pl.ds(i * rows, rows) for i in range(count)]
    return [pltpu.make_async_copy(source.at[p], target.at[p], sems.at[i]) for i, p in enumerate(pieces)]


def key_views(count):
    me = lax.axis_index("view")
    core = me & 1
    near, far = 2 * (me & 2) - 2, 4 - 2 * (me & 4)
    sources = (me, me + 1 - 2 * core, me + near, me - near, me - 1 + 2 * core, me + far, me - far)
    return [2 * lax.rem(s + count, count) for s in sources]


def bias_kernel(count, partners_ref, counts_ref, after_ref, bias_ref):
    bias_ref[...] = jnp.zeros_like(bias_ref)
    firsts = key_views(count)
    for qv in range(2):
        used = counts_ref[qv]
        named = [jnp.where(r < used, partners_ref[qv, r], -1) for r in range(ROUNDS)]
        for slot, first in enumerate(firsts):
            for kvw in range(2):
                if (slot in DIAGONAL or slot == 0) and (kvw == qv) == (slot == 0):
                    continue
                times = sum((n == first + kvw).astype(jnp.int32) for n in named)
                row = BIASES * qv + 2 * slot + kvw
                bias_ref[row : row + 1] = jnp.full((1, bias_ref.shape[1]), times.astype(jnp.float32))
    times = bias_ref[...]
    bias_ref[...] = jnp.where(times > 0, jnp.log2(jnp.maximum(times, 1.0)), MASKED)
    for qv in range(2):
        row = BIASES * qv + qv
        bias_ref[row : row + 1] = jnp.zeros((1, bias_ref.shape[1]), jnp.float32)


def biases(count, partners, counts, after):
    return pl.pallas_call(
        functools.partial(bias_kernel, count),
        out_shape=held((2 * BIASES, 2 * HD), jnp.float32),
        in_specs=[SMEM, SMEM, ANY],
        out_specs=VMEM,
        compiler_params=params(2),
        cost_estimate=COST,
        name="biases",
    )(partners, counts, after)


def project_kernel(x_hbm, wk_hbm, wv_hbm, wo_hbm, x_ref, kv_ref, half_ref, wk, wv, sems):
    half = half_ref.shape[0]
    mine = pl.ds(pl.multiple_of((lax.axis_index("view") & 1) * half, half), half)
    pairs = ((x_hbm, x_ref), (wk_hbm, wk), (wv_hbm, wv), (wo_hbm.at[mine], half_ref))
    loads = [pltpu.make_async_copy(source, target, sems.at[i]) for i, (source, target) in enumerate(pairs)]
    for copy in loads:
        copy.start()
    rows = x_ref.shape[0]
    loads[0].wait()
    loads[1].wait()
    kv_ref[:rows] = dot(x_ref[...], wk[...]).astype(jnp.bfloat16)
    loads[2].wait()
    kv_ref[rows:] = dot(x_ref[...], wv[...]).T.astype(jnp.bfloat16)
    loads[3].wait()


def project(x, w_key, w_value, w_out):
    rows, width = x.shape
    columns = w_key.shape[1]
    return pl.pallas_call(
        project_kernel,
        out_shape=(
            held(x.shape, x.dtype),
            held((rows + columns, rows), jnp.bfloat16),
            held((w_out.shape[0] // 2, w_out.shape[1]), w_out.dtype),
        ),
        in_specs=[HBM] * 4,
        out_specs=(VMEM,) * 3,
        scratch_shapes=[pltpu.VMEM((width, columns), jnp.bfloat16)] * 2 + [pltpu.SemaphoreType.DMA((4,))],
        compiler_params=params(8),
        cost_estimate=COST,
        name="project",
    )(*outside(x, w_key, w_value, w_out))


def ask_kernel(x_ref, wq_ref, after_ref, q_ref):
    q_ref[...] = (dot(x_ref[...], wq_ref[...]) * (HD ** (-0.5) * LOG2E)).astype(jnp.bfloat16)


def ask(x, w_query, after):
    return pl.pallas_call(
        ask_kernel,
        out_shape=held((x.shape[0], w_query.shape[1]), jnp.bfloat16),
        in_specs=[VMEM, VMEM, ANY],
        out_specs=VMEM,
        compiler_params=params(4),
        cost_estimate=COST,
        name="ask",
    )(x, w_query, after)


def attend_kernel(blocks, first, last, bias_ref, q_ref, *refs):
    count = len(blocks)
    kv_refs = refs[:count]
    refs = refs[count:]
    if not first:
        held_ref, held_tops_ref = refs[:2]
        refs = refs[2:]
    refs = refs[-1:] if last else refs[-2:]
    rows, columns = q_ref.shape
    tok, heads = rows // 2, columns // HD
    lane = lax.broadcasted_iota(jnp.int32, (tok, columns), 1)
    for qv in range(2):
        mine = slice(qv * tok, (qv + 1) * tok)
        q = q_ref[mine]
        apart = jnp.concatenate([jnp.where(lane // HD == h, q, jnp.zeros_like(q)) for h in range(heads)], axis=0)
        scores, biases, values = [], [], []
        for (slot, part, both), kv_ref in zip(blocks, kv_refs):
            base = part * (rows + columns)
            for kvw in (0, 1) if both else (qv,):
                span = slice(kvw * tok, (kvw + 1) * tok)
                keys = kv_ref[base + kvw * tok : base + (kvw + 1) * tok]
                scores.append(lax.dot_general(keys, apart, NT, preferred_element_type=jnp.float32))
                row = BIASES * qv + 2 * slot + kvw
                biases.append(jnp.concatenate([bias_ref[row : row + 1]] * heads, axis=1))
                values.append(kv_ref[base + rows : base + rows + columns, span])
        top = functools.reduce(jnp.maximum, [jnp.max(s, axis=0, keepdims=True) + b for s, b in zip(scores, biases)])
        if not first:
            old_top, old_total = held_tops_ref[2 * qv : 2 * qv + 1], held_tops_ref[2 * qv + 1 : 2 * qv + 2]
            top = jnp.maximum(top, old_top)
            scale = jnp.exp2(old_top - top)
        weights = [jnp.exp2(s - (top - b)) for s, b in zip(scores, biases)]
        total = jnp.sum(functools.reduce(jnp.add, weights), axis=0, keepdims=True)
        if not first:
            total = total + scale * old_total
        rounded = jnp.concatenate([w.astype(jnp.bfloat16) for w in weights], axis=0)
        values = jnp.concatenate(values, axis=1)
        finished = []
        for p in range(heads // 2):
            two = dot(values[2 * p * HD : 2 * (p + 1) * HD], rounded[:, 2 * p * tok : 2 * (p + 1) * tok])
            for h in (2 * p, 2 * p + 1):
                lanes = slice(h * tok, (h + 1) * tok)
                blended = two[(h - 2 * p) * HD : (h - 2 * p + 1) * HD, (h - 2 * p) * tok : (h - 2 * p + 1) * tok]
                at = slice((qv * heads + h) * HD, (qv * heads + h + 1) * HD)
                if not first:
                    blended = blended + scale[:, lanes] * held_ref[at]
                if last:
                    finished.append(blended / total[:, lanes])
                else:
                    refs[0][at] = blended
        if last:
            refs[0][mine] = jnp.concatenate(finished, axis=0).T.astype(jnp.bfloat16)
        else:
            refs[1][2 * qv : 2 * qv + 1] = top
            refs[1][2 * qv + 1 : 2 * qv + 2] = total


def attend(blocks, first, last, bias, q, kvs, state=(), *after):
    rows, columns = q.shape
    tok, heads = rows // 2, columns // HD
    if last:
        out = held((rows, columns), jnp.bfloat16)
    else:
        out = (
            held((2 * columns, tok), jnp.float32),
            held((4, heads * tok), jnp.float32),
        )
    return pl.pallas_call(
        functools.partial(attend_kernel, blocks, first, last),
        out_shape=out,
        in_specs=[VMEM] * (2 + len(kvs) + len(state)) + [ANY] * len(after),
        out_specs=VMEM if last else (VMEM, VMEM),
        compiler_params=params(16),
        cost_estimate=COST,
        name="attend",
    )(bias, q, *kvs, *state, *after)


def pick_kernel(a_ref, b_ref, *refs):
    out_ref = refs[-1]
    me = lax.axis_index("view")
    first = (me & 1) != ((me >> 1) & 1)

    @pl.when(first)
    def _():
        out_ref[...] = a_ref[...]

    @pl.when(jnp.logical_not(first))
    def _():
        out_ref[...] = b_ref[...]


def pick(a, b, *after):
    return pl.pallas_call(
        pick_kernel,
        out_shape=held(a.shape, a.dtype),
        in_specs=[VMEM] * 2 + [ANY] * len(after),
        out_specs=VMEM,
        compiler_params=params(2),
        cost_estimate=COST,
        name="pick",
    )(a, b, *after)


def stack_kernel(*refs):
    *piece_refs, _, out_ref = refs
    at = 0
    for ref in piece_refs:
        out_ref[at : at + ref.shape[0]] = ref[...]
        at += ref.shape[0]


def stack(*pieces, after):
    return pl.pallas_call(
        stack_kernel,
        out_shape=held((sum(p.shape[0] for p in pieces), pieces[0].shape[1]), pieces[0].dtype),
        in_specs=[VMEM] * len(pieces) + [ANY],
        out_specs=VMEM,
        compiler_params=params(2),
        cost_estimate=COST,
        name="stack",
    )(*pieces, after)


def turned(ref, tok, columns=slice(None)):
    head = lax.axis_index("head")
    part = tok // 4
    pieces = []
    for j in range(4):
        for view in range(2):
            start = pl.multiple_of(view * tok + jnp.bitwise_xor(head, j) * part, part)
            pieces.append(ref[pl.ds(start, part), columns])
    return jnp.concatenate(pieces, axis=0)


def lay_kernel(a0, a1, a2, a3, out_ref):
    tok = a0.shape[0] // 2
    block = a0.shape[1]
    half = block // 2
    core = lax.axis_index("view") & 1
    out_ref[:, :block] = turned(a0, tok)
    for i, a in enumerate((a1, a3, a2)):
        for k, which in enumerate((core, 1 - core)):
            at = block * (i + 1) + half * k
            out_ref[:, at : at + half] = turned(a, tok, pl.ds(pl.multiple_of(which * half, half), half))


def lay(*pieces):
    rows, columns = pieces[0].shape
    return pl.pallas_call(
        lay_kernel,
        out_shape=held((rows, 4 * columns), pieces[0].dtype),
        in_specs=[VMEM] * 4,
        out_specs=VMEM,
        compiler_params=params(4),
        cost_estimate=pl.CostEstimate(flops=20_000_000_000, bytes_accessed=1000, transcendentals=0),
        name="lay",
    )(*pieces)


def feed_kernel(x_ref, left_ref, o0, w1, w32, pair, win_ref, wback_ref, own_ref, r1, r2, r3):
    rows, width = x_ref.shape
    tok = rows // 2
    part = tok // 4
    half = w1.shape[0]
    blocks = (w1[...], w32[:half], w32[half:])
    right = [o0[...]] + [r for i, w in enumerate(blocks) for r in (w, pair[i * half : (i + 1) * half])]
    attention = dot(left_ref[...], jnp.concatenate(right, axis=0))
    y = turned(x_ref, tok).astype(jnp.float32) + attention
    normed = (y * lax.rsqrt(jnp.mean(y * y, axis=-1, keepdims=True) + 1e-06)).astype(jnp.bfloat16)
    hidden = jax.nn.gelu(dot(normed, win_ref[...])).astype(jnp.bfloat16)
    update = dot(hidden, wback_ref[...])
    own_ref[...] = attention[: 2 * part] + update[: 2 * part]
    for j, ref in ((1, r1), (2, r2), (3, r3)):
        ref[...] = update[2 * part * j : 2 * part * (j + 1)].astype(jnp.bfloat16)


def feed(x, left, w_outs, w_in, w_back):
    rows, width = x.shape
    piece = held((rows // 4, width), jnp.bfloat16)
    return pl.pallas_call(
        feed_kernel,
        out_shape=(held((rows // 4, width), jnp.float32), piece, piece, piece),
        in_specs=[VMEM] * 8,
        out_specs=(VMEM,) * 4,
        compiler_params=params(16),
        cost_estimate=COST,
        name="feed",
    )(x, left, *w_outs, w_in, w_back)


def gather_kernel(own_ref, r1, r2, r3, kept_ref, sent_ref):
    branch = lax.axis_index("branch")
    part = own_ref.shape[0] // 2
    half = part // 2
    for view in range(2):
        for side, ref in ((1 - branch, sent_ref), (branch, kept_ref)):
            rows = pl.ds(pl.multiple_of(view * part + side * half, half), half)
            total = own_ref[rows, :]
            for r in (r1, r2, r3):
                total = total + r[rows, :].astype(jnp.float32)
            ref[view * half : (view + 1) * half, :] = total.astype(ref.dtype)


def gather(own, received):
    rows, width = own.shape
    return pl.pallas_call(
        gather_kernel,
        out_shape=(
            held((rows // 2, width), jnp.float32),
            held((rows // 2, width), jnp.bfloat16),
        ),
        in_specs=[VMEM] * 4,
        out_specs=(VMEM, VMEM),
        compiler_params=params(2),
        cost_estimate=COST,
        name="gather",
    )(own, *received)


def guide_kernel(guidance_ref, kept_ref, other_ref, out_ref):
    strength = guidance_ref[0]
    weight = jnp.where(lax.axis_index("branch") == 0, strength, 1.0 - strength)
    kept = kept_ref[...]
    guided = weight * kept + (1.0 - weight) * other_ref[...].astype(jnp.float32)
    out_ref[...] = guided.astype(out_ref.dtype)


def guide(guidance, kept, other):
    return pl.pallas_call(
        guide_kernel,
        out_shape=jax.ShapeDtypeStruct(other.shape, jnp.bfloat16),
        in_specs=[SMEM, VMEM, VMEM],
        out_specs=VMEM,
        compiler_params=params(2),
        cost_estimate=COST,
        name="guide",
    )(guidance, kept, other)


def on_device(tokens, partners, counts, w_query, w_key, w_value, w_out, w_in, w_back, guidance):
    per_device, tok, width = tokens.shape[1:]
    x = tokens[0].reshape(per_device * tok, width)
    count = lax.axis_size("view")

    x, kv, w_half = project(x, w_key, w_value, w_out)

    near = [matched(count, 2, parity)(kv) for parity in (1, 0)]
    across = flipped("view", count, 4)(kv)
    far = (across, onward(count)(across))
    w_1 = flipped("head", 4, 1)(w_half)
    w_32 = flipped("head", 4, 3)(stack(w_half, w_1, after=x))
    q = ask(x, w_query, x)
    bias = biases(count, partners.T, counts, x)
    state = attend(((0, 0, True), (2, 0, False), (3, 0, False)), True, False, bias, q, (kv, *near))
    other_core = flipped("view", count, 1)
    other, cross = other_core(kv), other_core(pick(*near, *far, state[1]))
    state = attend(((1, 0, True), (5, 0, False), (6, 0, False)), False, False, bias, q, (other, *far), state, w_32)
    attended = attend(((4, 0, True),), False, True, bias, q, (cross,), state)
    w_pair = other_core(stack(w_1, w_32, after=attended))

    pieces = [attended] + [flipped("head", 4, j)(attended) for j in (1, 2, 3)]
    own, *outgoing = feed(x, lay(*pieces), (w_out, w_1, w_32, w_pair), w_in, w_back)
    received = [flipped("head", 4, j)(r) for j, r in zip((1, 2, 3), outgoing)]
    kept, sent = gather(own, received)
    other = flipped("branch", 2, 1)(sent)
    return guide(guidance, kept, other).reshape(per_device, -1, width)


def solution(mesh):
    placed = (
        P("branch", "view", None, None),
        P(None, "view"),
        P("view"),
        P(None, "head"),
        P(None, "head"),
        P(None, "head"),
        P("head", None),
        P(None, "head"),
        P("head", None),
        P(),
    )
    return jax.shard_map(
        on_device,
        mesh=mesh,
        in_specs=placed,
        out_specs=P("view", ("head", "branch"), None),
        check_vma=False,
    )
```

```python
import functools

import jax
import jax.numpy as jnp
from jax import lax
from jax.experimental import pallas as pl
from jax.experimental.pallas import tpu as pltpu
from jax.sharding import PartitionSpec as P

HD = 64
ROUNDS = 8
BIASES = 16
DIAGONAL = (2, 3, 5, 6)
MASKED = -1e30
LOG2E = 1.4426950408889634

NT = (((1,), (1,)), ((), ()))
VMEM = pl.BlockSpec(memory_space=pltpu.VMEM)
SMEM = pl.BlockSpec(memory_space=pltpu.SMEM)
HBM = pl.BlockSpec(memory_space=pltpu.HBM)
ANY = pl.BlockSpec(memory_space=pl.ANY)


def params(mib):
    return pltpu.CompilerParams(vmem_limit_bytes=int(mib * 1024 * 1024))


def matched(count, apart, parity):
    route = []
    for low in range(count):
        if (low // apart) % 2 == parity:
            high = (low + apart) % count
            route += [(low, high), (high, low)]
    return functools.partial(lax.ppermute, axis_name="view", perm=route)


def onward(count):
    route = [(i, (i + 8 - 4 * (i & 4)) % count) for i in range(count)]
    return functools.partial(lax.ppermute, axis_name="view", perm=route)


def flipped(axis, count, bits):
    return functools.partial(lax.ppermute, axis_name=axis, perm=[(i, i ^ bits) for i in range(count)])


def held(shape, dtype):
    return pltpu.VMEM(shape, dtype)


def outside(*arrays):
    return tuple(pltpu.with_memory_space_constraint(a, pltpu.HBM) for a in arrays)


COST = pl.CostEstimate(flops=1000, bytes_accessed=1000, transcendentals=0)


def dot(a, b):
    return jnp.dot(a, b, preferred_element_type=jnp.float32)


def chunked(source, target, sems, count):
    rows = source.shape[0] // count
    pieces = [pl.ds(i * rows, rows) for i in range(count)]
    return [pltpu.make_async_copy(source.at[p], target.at[p], sems.at[i]) for i, p in enumerate(pieces)]


def key_views(count):
    me = lax.axis_index("view")
    core = me & 1
    near, far = 2 * (me & 2) - 2, 4 - 2 * (me & 4)
    sources = (me, me + 1 - 2 * core, me + near, me - near, me - 1 + 2 * core, me + far, me - far)
    return [2 * lax.rem(s + count, count) for s in sources]


def bias_kernel(count, partners_ref, counts_ref, after_ref, bias_ref):
    bias_ref[...] = jnp.zeros_like(bias_ref)
    firsts = key_views(count)
    for qv in range(2):
        used = counts_ref[qv]
        named = [jnp.where(r < used, partners_ref[qv, r], -1) for r in range(ROUNDS)]
        for slot, first in enumerate(firsts):
            for kvw in range(2):
                if (slot in DIAGONAL or slot == 0) and (kvw == qv) == (slot == 0):
                    continue
                times = sum((n == first + kvw).astype(jnp.int32) for n in named)
                row = BIASES * qv + 2 * slot + kvw
                bias_ref[row : row + 1] = jnp.full((1, bias_ref.shape[1]), times.astype(jnp.float32))
    times = bias_ref[...]
    bias_ref[...] = jnp.where(times > 0, jnp.log2(jnp.maximum(times, 1.0)), MASKED)
    for qv in range(2):
        row = BIASES * qv + qv
        bias_ref[row : row + 1] = jnp.zeros((1, bias_ref.shape[1]), jnp.float32)


def biases(count, partners, counts, after):
    return pl.pallas_call(
        functools.partial(bias_kernel, count),
        out_shape=held((2 * BIASES, 2 * HD), jnp.float32),
        in_specs=[SMEM, SMEM, ANY],
        out_specs=VMEM,
        compiler_params=params(2),
        cost_estimate=COST,
        name="biases",
    )(partners, counts, after)


def project_kernel(x_hbm, wk_hbm, wv_hbm, wo_hbm, x_ref, kv_ref, half_ref, wk, wv, sems):
    half = half_ref.shape[0]
    mine = pl.ds(pl.multiple_of((lax.axis_index("view") & 1) * half, half), half)
    pairs = ((x_hbm, x_ref), (wk_hbm, wk), (wv_hbm, wv), (wo_hbm.at[mine], half_ref))
    loads = [pltpu.make_async_copy(source, target, sems.at[i]) for i, (source, target) in enumerate(pairs)]
    for copy in loads:
        copy.start()
    rows = x_ref.shape[0]
    loads[0].wait()
    loads[1].wait()
    kv_ref[:rows] = dot(x_ref[...], wk[...]).astype(jnp.bfloat16)
    loads[2].wait()
    kv_ref[rows:] = dot(x_ref[...], wv[...]).T.astype(jnp.bfloat16)
    loads[3].wait()


def project(x, w_key, w_value, w_out):
    rows, width = x.shape
    columns = w_key.shape[1]
    return pl.pallas_call(
        project_kernel,
        out_shape=(
            held(x.shape, x.dtype),
            held((rows + columns, rows), jnp.bfloat16),
            held((w_out.shape[0] // 2, w_out.shape[1]), w_out.dtype),
        ),
        in_specs=[HBM] * 4,
        out_specs=(VMEM,) * 3,
        scratch_shapes=[pltpu.VMEM((width, columns), jnp.bfloat16)] * 2 + [pltpu.SemaphoreType.DMA((4,))],
        compiler_params=params(8),
        cost_estimate=COST,
        name="project",
    )(*outside(x, w_key, w_value, w_out))


def ask_kernel(x_ref, wq_ref, after_ref, q_ref):
    q_ref[...] = (dot(x_ref[...], wq_ref[...]) * (HD ** (-0.5) * LOG2E)).astype(jnp.bfloat16)


def ask(x, w_query, after):
    return pl.pallas_call(
        ask_kernel,
        out_shape=held((x.shape[0], w_query.shape[1]), jnp.bfloat16),
        in_specs=[VMEM, VMEM, ANY],
        out_specs=VMEM,
        compiler_params=params(4),
        cost_estimate=COST,
        name="ask",
    )(x, w_query, after)


def attend_kernel(blocks, first, last, bias_ref, q_ref, *refs):
    refs, kv_refs = list(refs), []
    for _, part, _ in blocks:
        kv_refs.append(refs.pop(0) if part is not None else (refs.pop(0), refs.pop(0)))
    if not first:
        held_ref, held_tops_ref = refs[:2]
        refs = refs[2:]
    refs = refs[-1:] if last else refs[-2:]
    rows, columns = q_ref.shape
    tok, heads = rows // 2, columns // HD
    lane = lax.broadcasted_iota(jnp.int32, (tok, columns), 1)
    for qv in range(2):
        mine = slice(qv * tok, (qv + 1) * tok)
        q = q_ref[mine]
        apart = jnp.concatenate([jnp.where(lane // HD == h, q, jnp.zeros_like(q)) for h in range(heads)], axis=0)
        scores, biases, values = [], [], []
        for (slot, part, both), kv_ref in zip(blocks, kv_refs):
            base = (part or 0) * (rows + columns)
            k_ref, v_ref, v_base = (kv_ref, kv_ref, base + rows) if part is not None else (*kv_ref, 0)
            for kvw in (0, 1) if both else (qv,):
                span = slice(kvw * tok, (kvw + 1) * tok)
                keys = k_ref[base + kvw * tok : base + (kvw + 1) * tok]
                scores.append(lax.dot_general(keys, apart, NT, preferred_element_type=jnp.float32))
                row = BIASES * qv + 2 * slot + kvw
                biases.append(jnp.concatenate([bias_ref[row : row + 1]] * heads, axis=1))
                values.append(v_ref[v_base : v_base + columns, span])
        top = functools.reduce(jnp.maximum, [jnp.max(s, axis=0, keepdims=True) + b for s, b in zip(scores, biases)])
        if not first:
            old_top, old_total = held_tops_ref[2 * qv : 2 * qv + 1], held_tops_ref[2 * qv + 1 : 2 * qv + 2]
            top = jnp.maximum(top, old_top)
            scale = jnp.exp2(old_top - top)
        weights = [jnp.exp2(s - (top - b)) for s, b in zip(scores, biases)]
        total = jnp.sum(functools.reduce(jnp.add, weights), axis=0, keepdims=True)
        if not first:
            total = total + scale * old_total
        rounded = jnp.concatenate([w.astype(jnp.bfloat16) for w in weights], axis=0)
        values = jnp.concatenate(values, axis=1)
        finished = []
        for p in range(heads // 2):
            two = dot(values[2 * p * HD : 2 * (p + 1) * HD], rounded[:, 2 * p * tok : 2 * (p + 1) * tok])
            for h in (2 * p, 2 * p + 1):
                lanes = slice(h * tok, (h + 1) * tok)
                blended = two[(h - 2 * p) * HD : (h - 2 * p + 1) * HD, (h - 2 * p) * tok : (h - 2 * p + 1) * tok]
                at = slice((qv * heads + h) * HD, (qv * heads + h + 1) * HD)
                if not first:
                    blended = blended + scale[:, lanes] * held_ref[at]
                if last:
                    finished.append(blended / total[:, lanes])
                else:
                    refs[0][at] = blended
        if last:
            refs[0][mine] = jnp.concatenate(finished, axis=0).T.astype(jnp.bfloat16)
        else:
            refs[1][2 * qv : 2 * qv + 1] = top
            refs[1][2 * qv + 1 : 2 * qv + 2] = total


def attend(blocks, first, last, bias, q, kvs, state=(), *after):
    rows, columns = q.shape
    tok, heads = rows // 2, columns // HD
    if last:
        out = held((rows, columns), jnp.bfloat16)
    else:
        out = (
            held((2 * columns, tok), jnp.float32),
            held((4, heads * tok), jnp.float32),
        )
    return pl.pallas_call(
        functools.partial(attend_kernel, blocks, first, last),
        out_shape=out,
        in_specs=[VMEM] * (2 + len(kvs) + len(state)) + [ANY] * len(after),
        out_specs=VMEM if last else (VMEM, VMEM),
        compiler_params=params(16),
        cost_estimate=COST,
        name="attend",
    )(bias, q, *kvs, *state, *after)


def pick_kernel(a_ref, b_ref, *refs):
    keys_ref, values_ref = refs[-2:]
    rows = keys_ref.shape[0]
    me = lax.axis_index("view")
    first = (me & 1) != ((me >> 1) & 1)

    @pl.when(first)
    def _():
        keys_ref[...] = a_ref[:rows]
        values_ref[...] = a_ref[rows:]

    @pl.when(jnp.logical_not(first))
    def _():
        keys_ref[...] = b_ref[:rows]
        values_ref[...] = b_ref[rows:]


def pick(a, b, *after):
    return pl.pallas_call(
        pick_kernel,
        out_shape=(held((a.shape[0] // 2, a.shape[1]), a.dtype),) * 2,
        in_specs=[VMEM] * 2 + [ANY] * len(after),
        out_specs=(VMEM,) * 2,
        compiler_params=params(2),
        cost_estimate=COST,
        name="pick",
    )(a, b, *after)


def stack_kernel(*refs):
    *piece_refs, _, out_ref = refs
    at = 0
    for ref in piece_refs:
        out_ref[at : at + ref.shape[0]] = ref[...]
        at += ref.shape[0]


def stack(*pieces, after):
    return pl.pallas_call(
        stack_kernel,
        out_shape=held((sum(p.shape[0] for p in pieces), pieces[0].shape[1]), pieces[0].dtype),
        in_specs=[VMEM] * len(pieces) + [ANY],
        out_specs=VMEM,
        compiler_params=params(2),
        cost_estimate=COST,
        name="stack",
    )(*pieces, after)


def turned(ref, tok, columns=slice(None)):
    head = lax.axis_index("head")
    part = tok // 4
    pieces = []
    for j in range(4):
        for view in range(2):
            start = pl.multiple_of(view * tok + jnp.bitwise_xor(head, j) * part, part)
            pieces.append(ref[pl.ds(start, part), columns])
    return jnp.concatenate(pieces, axis=0)


def lay_kernel(a0, a1, a2, a3, out_ref):
    tok = a0.shape[0] // 2
    block = a0.shape[1]
    half = block // 2
    core = lax.axis_index("view") & 1
    out_ref[:, :block] = turned(a0, tok)
    for i, a in enumerate((a1, a3, a2)):
        for k, which in enumerate((core, 1 - core)):
            at = block * (i + 1) + half * k
            out_ref[:, at : at + half] = turned(a, tok, pl.ds(pl.multiple_of(which * half, half), half))


def lay(*pieces):
    rows, columns = pieces[0].shape
    return pl.pallas_call(
        lay_kernel,
        out_shape=held((rows, 4 * columns), pieces[0].dtype),
        in_specs=[VMEM] * 4,
        out_specs=VMEM,
        compiler_params=params(4),
        cost_estimate=pl.CostEstimate(flops=20_000_000_000, bytes_accessed=1000, transcendentals=0),
        name="lay",
    )(*pieces)


def feed_kernel(x_ref, left_ref, o0, w1, w32, pair, win_ref, wback_ref, own_ref, r1, r2, r3):
    rows, width = x_ref.shape
    tok = rows // 2
    part = tok // 4
    half = w1.shape[0]
    blocks = (w1[...], w32[:half], w32[half:])
    right = [o0[...]] + [r for i, w in enumerate(blocks) for r in (w, pair[i * half : (i + 1) * half])]
    attention = dot(left_ref[...], jnp.concatenate(right, axis=0))
    y = turned(x_ref, tok).astype(jnp.float32) + attention
    normed = (y * lax.rsqrt(jnp.mean(y * y, axis=-1, keepdims=True) + 1e-06)).astype(jnp.bfloat16)
    hidden = jax.nn.gelu(dot(normed, win_ref[...])).astype(jnp.bfloat16)
    update = dot(hidden, wback_ref[...])
    own_ref[...] = attention[: 2 * part] + update[: 2 * part]
    for j, ref in ((1, r1), (2, r2), (3, r3)):
        ref[...] = update[2 * part * j : 2 * part * (j + 1)].astype(jnp.bfloat16)


def feed(x, left, w_outs, w_in, w_back):
    rows, width = x.shape
    piece = held((rows // 4, width), jnp.bfloat16)
    return pl.pallas_call(
        feed_kernel,
        out_shape=(held((rows // 4, width), jnp.float32), piece, piece, piece),
        in_specs=[VMEM] * 8,
        out_specs=(VMEM,) * 4,
        compiler_params=params(16),
        cost_estimate=COST,
        name="feed",
    )(x, left, *w_outs, w_in, w_back)


def gather_kernel(own_ref, r1, r2, r3, kept_ref, sent_ref):
    branch = lax.axis_index("branch")
    part = own_ref.shape[0] // 2
    half = part // 2
    for view in range(2):
        for side, ref in ((1 - branch, sent_ref), (branch, kept_ref)):
            rows = pl.ds(pl.multiple_of(view * part + side * half, half), half)
            total = own_ref[rows, :]
            for r in (r1, r2, r3):
                total = total + r[rows, :].astype(jnp.float32)
            ref[view * half : (view + 1) * half, :] = total.astype(ref.dtype)


def gather(own, received):
    rows, width = own.shape
    return pl.pallas_call(
        gather_kernel,
        out_shape=(
            held((rows // 2, width), jnp.float32),
            held((rows // 2, width), jnp.bfloat16),
        ),
        in_specs=[VMEM] * 4,
        out_specs=(VMEM, VMEM),
        compiler_params=params(2),
        cost_estimate=COST,
        name="gather",
    )(own, *received)


def guide_kernel(guidance_ref, kept_ref, other_ref, out_ref):
    strength = guidance_ref[0]
    weight = jnp.where(lax.axis_index("branch") == 0, strength, 1.0 - strength)
    kept = kept_ref[...]
    guided = weight * kept + (1.0 - weight) * other_ref[...].astype(jnp.float32)
    out_ref[...] = guided.astype(out_ref.dtype)


def guide(guidance, kept, other):
    return pl.pallas_call(
        guide_kernel,
        out_shape=jax.ShapeDtypeStruct(other.shape, jnp.bfloat16),
        in_specs=[SMEM, VMEM, VMEM],
        out_specs=VMEM,
        compiler_params=params(2),
        cost_estimate=COST,
        name="guide",
    )(guidance, kept, other)


def on_device(tokens, partners, counts, w_query, w_key, w_value, w_out, w_in, w_back, guidance):
    per_device, tok, width = tokens.shape[1:]
    x = tokens[0].reshape(per_device * tok, width)
    count = lax.axis_size("view")

    x, kv, w_half = project(x, w_key, w_value, w_out)

    near = [matched(count, 2, parity)(kv) for parity in (1, 0)]
    across = flipped("view", count, 4)(kv)
    far = (across, onward(count)(across))
    w_1 = flipped("head", 4, 1)(w_half)
    w_32 = flipped("head", 4, 3)(stack(w_half, w_1, after=x))
    q = ask(x, w_query, x)
    bias = biases(count, partners.T, counts, x)
    state = attend(((0, 0, True),), True, False, bias, q, (kv,))
    other_core = flipped("view", count, 1)
    other = other_core(kv)
    cross = [other_core(p) for p in pick(*near, state[1])]
    state = attend(((1, 0, True), (2, 0, False), (3, 0, False)), False, False, bias, q, (other, *near), state)
    attended = attend(((4, None, True), (5, 0, False), (6, 0, False)), False, True, bias, q, (*cross, *far), state)
    w_pair = other_core(stack(w_1, w_32, after=attended))

    pieces = [attended] + [flipped("head", 4, j)(attended) for j in (1, 2, 3)]
    own, *outgoing = feed(x, lay(*pieces), (w_out, w_1, w_32, w_pair), w_in, w_back)
    received = [flipped("head", 4, j)(r) for j, r in zip((1, 2, 3), outgoing)]
    kept, sent = gather(own, received)
    other = flipped("branch", 2, 1)(sent)
    return guide(guidance, kept, other).reshape(per_device, -1, width)


def solution(mesh):
    placed = (
        P("branch", "view", None, None),
        P(None, "view"),
        P("view"),
        P(None, "head"),
        P(None, "head"),
        P(None, "head"),
        P("head", None),
        P(None, "head"),
        P("head", None),
        P(),
    )
    return jax.shard_map(
        on_device,
        mesh=mesh,
        in_specs=placed,
        out_specs=P("view", ("head", "branch"), None),
        check_vma=False,
    )
```

```python
import functools

import jax
import jax.numpy as jnp
from jax import lax
from jax.experimental import pallas as pl
from jax.experimental.pallas import tpu as pltpu
from jax.sharding import PartitionSpec as P

HD = 64
ROUNDS = 8
BIASES = 16
DIAGONAL = (2, 3, 5, 6)
MASKED = -1e30
LOG2E = 1.4426950408889634

NT = (((1,), (1,)), ((), ()))
VMEM = pl.BlockSpec(memory_space=pltpu.VMEM)
SMEM = pl.BlockSpec(memory_space=pltpu.SMEM)
HBM = pl.BlockSpec(memory_space=pltpu.HBM)
ANY = pl.BlockSpec(memory_space=pl.ANY)


def params(mib):
    return pltpu.CompilerParams(vmem_limit_bytes=int(mib * 1024 * 1024))


def matched(count, apart, parity):
    route = []
    for low in range(count):
        if (low // apart) % 2 == parity:
            high = (low + apart) % count
            route += [(low, high), (high, low)]
    return functools.partial(lax.ppermute, axis_name="view", perm=route)


def onward(count):
    route = [(i, (i + 8 - 4 * (i & 4)) % count) for i in range(count)]
    return functools.partial(lax.ppermute, axis_name="view", perm=route)


def flipped(axis, count, bits):
    return functools.partial(lax.ppermute, axis_name=axis, perm=[(i, i ^ bits) for i in range(count)])


def held(shape, dtype):
    return pltpu.VMEM(shape, dtype)


def outside(*arrays):
    return tuple(pltpu.with_memory_space_constraint(a, pltpu.HBM) for a in arrays)


COST = pl.CostEstimate(flops=1000, bytes_accessed=1000, transcendentals=0)


def dot(a, b):
    return jnp.dot(a, b, preferred_element_type=jnp.float32)


def chunked(source, target, sems, count):
    rows = source.shape[0] // count
    pieces = [pl.ds(i * rows, rows) for i in range(count)]
    return [pltpu.make_async_copy(source.at[p], target.at[p], sems.at[i]) for i, p in enumerate(pieces)]


def key_views(count):
    me = lax.axis_index("view")
    core = me & 1
    near, far = 2 * (me & 2) - 2, 4 - 2 * (me & 4)
    sources = (me, me + 1 - 2 * core, me + near, me - near, me - 1 + 2 * core, me + far, me - far)
    return [2 * lax.rem(s + count, count) for s in sources]


def bias_kernel(count, partners_ref, counts_ref, after_ref, bias_ref):
    bias_ref[...] = jnp.zeros_like(bias_ref)
    firsts = key_views(count)
    for qv in range(2):
        used = counts_ref[qv]
        named = [jnp.where(r < used, partners_ref[qv, r], -1) for r in range(ROUNDS)]
        for slot, first in enumerate(firsts):
            for kvw in range(2):
                if (slot in DIAGONAL or slot == 0) and (kvw == qv) == (slot == 0):
                    continue
                times = sum((n == first + kvw).astype(jnp.int32) for n in named)
                row = BIASES * qv + 2 * slot + kvw
                bias_ref[row : row + 1] = jnp.full((1, bias_ref.shape[1]), times.astype(jnp.float32))
    times = bias_ref[...]
    bias_ref[...] = jnp.where(times > 0, jnp.log2(jnp.maximum(times, 1.0)), MASKED)
    for qv in range(2):
        row = BIASES * qv + qv
        bias_ref[row : row + 1] = jnp.zeros((1, bias_ref.shape[1]), jnp.float32)


def biases(count, partners, counts, after):
    return pl.pallas_call(
        functools.partial(bias_kernel, count),
        out_shape=held((2 * BIASES, 2 * HD), jnp.float32),
        in_specs=[SMEM, SMEM, ANY],
        out_specs=VMEM,
        compiler_params=params(2),
        cost_estimate=COST,
        name="biases",
    )(partners, counts, after)


def project_kernel(x_hbm, wk_hbm, wv_hbm, wo_hbm, x_ref, kv_ref, half_ref, wk, wv, sems):
    half = half_ref.shape[0]
    mine = pl.ds(pl.multiple_of((lax.axis_index("view") & 1) * half, half), half)
    pairs = ((x_hbm, x_ref), (wk_hbm, wk), (wv_hbm, wv), (wo_hbm.at[mine], half_ref))
    loads = [pltpu.make_async_copy(source, target, sems.at[i]) for i, (source, target) in enumerate(pairs)]
    for copy in loads:
        copy.start()
    rows = x_ref.shape[0]
    loads[0].wait()
    loads[1].wait()
    kv_ref[:rows] = dot(x_ref[...], wk[...]).astype(jnp.bfloat16)
    loads[2].wait()
    kv_ref[rows:] = dot(x_ref[...], wv[...]).T.astype(jnp.bfloat16)
    loads[3].wait()


def project(x, w_key, w_value, w_out):
    rows, width = x.shape
    columns = w_key.shape[1]
    return pl.pallas_call(
        project_kernel,
        out_shape=(
            held(x.shape, x.dtype),
            held((rows + columns, rows), jnp.bfloat16),
            held((w_out.shape[0] // 2, w_out.shape[1]), w_out.dtype),
        ),
        in_specs=[HBM] * 4,
        out_specs=(VMEM,) * 3,
        scratch_shapes=[pltpu.VMEM((width, columns), jnp.bfloat16)] * 2 + [pltpu.SemaphoreType.DMA((4,))],
        compiler_params=params(8),
        cost_estimate=COST,
        name="project",
    )(*outside(x, w_key, w_value, w_out))


def ask_kernel(x_ref, wq_ref, after_ref, q_ref):
    q_ref[...] = (dot(x_ref[...], wq_ref[...]) * (HD ** (-0.5) * LOG2E)).astype(jnp.bfloat16)


def ask(x, w_query, after):
    return pl.pallas_call(
        ask_kernel,
        out_shape=held((x.shape[0], w_query.shape[1]), jnp.bfloat16),
        in_specs=[VMEM, VMEM, ANY],
        out_specs=VMEM,
        compiler_params=params(4),
        cost_estimate=COST,
        name="ask",
    )(x, w_query, after)


def attend_kernel(blocks, first, last, bias_ref, q_ref, *refs):
    refs, kv_refs = list(refs), []
    for _, part, _ in blocks:
        kv_refs.append(refs.pop(0) if part is not None else (refs.pop(0), refs.pop(0)))
    if not first:
        held_ref, held_tops_ref = refs[:2]
        refs = refs[2:]
    refs = refs[-1:] if last else refs[-2:]
    rows, columns = q_ref.shape
    tok, heads = rows // 2, columns // HD
    lane = lax.broadcasted_iota(jnp.int32, (tok, columns), 1)
    for qv in range(2):
        mine = slice(qv * tok, (qv + 1) * tok)
        q = q_ref[mine]
        apart = jnp.concatenate([jnp.where(lane // HD == h, q, jnp.zeros_like(q)) for h in range(heads)], axis=0)
        scores, biases, values = [], [], []
        for (slot, part, both), kv_ref in zip(blocks, kv_refs):
            base = (part or 0) * (rows + columns)
            k_ref, v_ref, v_base = (kv_ref, kv_ref, base + rows) if part is not None else (*kv_ref, 0)
            for kvw in (0, 1) if both else (qv,):
                span = slice(kvw * tok, (kvw + 1) * tok)
                keys = k_ref[base + kvw * tok : base + (kvw + 1) * tok]
                scores.append(lax.dot_general(keys, apart, NT, preferred_element_type=jnp.float32))
                row = BIASES * qv + 2 * slot + kvw
                biases.append(jnp.concatenate([bias_ref[row : row + 1]] * heads, axis=1))
                values.append(v_ref[v_base : v_base + columns, span])
        top = functools.reduce(jnp.maximum, [jnp.max(s, axis=0, keepdims=True) + b for s, b in zip(scores, biases)])
        if not first:
            old_top, old_total = held_tops_ref[2 * qv : 2 * qv + 1], held_tops_ref[2 * qv + 1 : 2 * qv + 2]
            top = jnp.maximum(top, old_top)
            scale = jnp.exp2(old_top - top)
        weights = [jnp.exp2(s - (top - b)) for s, b in zip(scores, biases)]
        total = jnp.sum(functools.reduce(jnp.add, weights), axis=0, keepdims=True)
        if not first:
            total = total + scale * old_total
        rounded = jnp.concatenate([w.astype(jnp.bfloat16) for w in weights], axis=0)
        values = jnp.concatenate(values, axis=1)
        finished = []
        for p in range(heads // 2):
            two = dot(values[2 * p * HD : 2 * (p + 1) * HD], rounded[:, 2 * p * tok : 2 * (p + 1) * tok])
            for h in (2 * p, 2 * p + 1):
                lanes = slice(h * tok, (h + 1) * tok)
                blended = two[(h - 2 * p) * HD : (h - 2 * p + 1) * HD, (h - 2 * p) * tok : (h - 2 * p + 1) * tok]
                at = slice((qv * heads + h) * HD, (qv * heads + h + 1) * HD)
                if not first:
                    blended = blended + scale[:, lanes] * held_ref[at]
                if last:
                    finished.append(blended / total[:, lanes])
                else:
                    refs[0][at] = blended
        if last:
            refs[0][mine] = jnp.concatenate(finished, axis=0).T.astype(jnp.bfloat16)
        else:
            refs[1][2 * qv : 2 * qv + 1] = top
            refs[1][2 * qv + 1 : 2 * qv + 2] = total


def attend(blocks, first, last, bias, q, kvs, state=(), *after):
    rows, columns = q.shape
    tok, heads = rows // 2, columns // HD
    if last:
        out = held((rows, columns), jnp.bfloat16)
    else:
        out = (
            held((2 * columns, tok), jnp.float32),
            held((4, heads * tok), jnp.float32),
        )
    return pl.pallas_call(
        functools.partial(attend_kernel, blocks, first, last),
        out_shape=out,
        in_specs=[VMEM] * (2 + len(kvs) + len(state)) + [ANY] * len(after),
        out_specs=VMEM if last else (VMEM, VMEM),
        compiler_params=params(16),
        cost_estimate=COST,
        name="attend",
    )(bias, q, *kvs, *state, *after)


def pick_kernel(a_ref, b_ref, *refs):
    keys_ref, values_ref = refs[-2:]
    rows = keys_ref.shape[0]
    me = lax.axis_index("view")
    first = (me & 1) != ((me >> 1) & 1)

    @pl.when(first)
    def _():
        keys_ref[...] = a_ref[:rows]
        values_ref[...] = a_ref[rows:]

    @pl.when(jnp.logical_not(first))
    def _():
        keys_ref[...] = b_ref[:rows]
        values_ref[...] = b_ref[rows:]


def pick(a, b, *after):
    return pl.pallas_call(
        pick_kernel,
        out_shape=(held((a.shape[0] // 2, a.shape[1]), a.dtype),) * 2,
        in_specs=[VMEM] * 2 + [ANY] * len(after),
        out_specs=(VMEM,) * 2,
        compiler_params=params(2),
        cost_estimate=COST,
        name="pick",
    )(a, b, *after)


def stack_kernel(pieces, *refs):
    out_ref = refs[-1]
    at = 0
    for ref in refs[:pieces]:
        out_ref[at : at + ref.shape[0]] = ref[...]
        at += ref.shape[0]


def stack(*pieces, after=()):
    return pl.pallas_call(
        functools.partial(stack_kernel, len(pieces)),
        out_shape=held((sum(p.shape[0] for p in pieces), pieces[0].shape[1]), pieces[0].dtype),
        in_specs=[VMEM] * len(pieces) + [ANY] * len(after),
        out_specs=VMEM,
        compiler_params=params(2),
        cost_estimate=COST,
        name="stack",
    )(*pieces, *after)


def turned(ref, tok, columns=slice(None)):
    head = lax.axis_index("head")
    part = tok // 4
    pieces = []
    for j in range(4):
        for view in range(2):
            start = pl.multiple_of(view * tok + jnp.bitwise_xor(head, j) * part, part)
            pieces.append(ref[pl.ds(start, part), columns])
    return jnp.concatenate(pieces, axis=0)


def lay_kernel(a0, a1, a2, a3, out_ref):
    tok = a0.shape[0] // 2
    block = a0.shape[1]
    half = block // 2
    core = lax.axis_index("view") & 1
    out_ref[:, :block] = turned(a0, tok)
    for i, a in enumerate((a1, a3, a2)):
        for k, which in enumerate((core, 1 - core)):
            at = block * (i + 1) + half * k
            out_ref[:, at : at + half] = turned(a, tok, pl.ds(pl.multiple_of(which * half, half), half))


def lay(*pieces):
    rows, columns = pieces[0].shape
    return pl.pallas_call(
        lay_kernel,
        out_shape=held((rows, 4 * columns), pieces[0].dtype),
        in_specs=[VMEM] * 4,
        out_specs=VMEM,
        compiler_params=params(4),
        cost_estimate=pl.CostEstimate(flops=20_000_000_000, bytes_accessed=1000, transcendentals=0),
        name="lay",
    )(*pieces)


def feed_kernel(x_ref, left_ref, o0, w1, w32, pair, win_ref, wback_ref, own_ref, r1, r2, r3):
    rows, width = x_ref.shape
    tok = rows // 2
    part = tok // 4
    half = w1.shape[0]
    blocks = (w1[...], w32[:half], w32[half:])
    right = [o0[...]] + [r for i, w in enumerate(blocks) for r in (w, pair[i * half : (i + 1) * half])]
    attention = dot(left_ref[...], jnp.concatenate(right, axis=0))
    y = turned(x_ref, tok).astype(jnp.float32) + attention
    normed = (y * lax.rsqrt(jnp.mean(y * y, axis=-1, keepdims=True) + 1e-06)).astype(jnp.bfloat16)
    hidden = jax.nn.gelu(dot(normed, win_ref[...])).astype(jnp.bfloat16)
    update = dot(hidden, wback_ref[...])
    own_ref[...] = attention[: 2 * part] + update[: 2 * part]
    for j, ref in ((1, r1), (2, r2), (3, r3)):
        ref[...] = update[2 * part * j : 2 * part * (j + 1)].astype(jnp.bfloat16)


def feed(x, left, w_outs, w_in, w_back):
    rows, width = x.shape
    piece = held((rows // 4, width), jnp.bfloat16)
    return pl.pallas_call(
        feed_kernel,
        out_shape=(held((rows // 4, width), jnp.float32), piece, piece, piece),
        in_specs=[VMEM] * 8,
        out_specs=(VMEM,) * 4,
        compiler_params=params(16),
        cost_estimate=COST,
        name="feed",
    )(x, left, *w_outs, w_in, w_back)


def gather_kernel(own_ref, r1, r2, r3, kept_ref, sent_ref):
    branch = lax.axis_index("branch")
    part = own_ref.shape[0] // 2
    half = part // 2
    for view in range(2):
        for side, ref in ((1 - branch, sent_ref), (branch, kept_ref)):
            rows = pl.ds(pl.multiple_of(view * part + side * half, half), half)
            total = own_ref[rows, :]
            for r in (r1, r2, r3):
                total = total + r[rows, :].astype(jnp.float32)
            ref[view * half : (view + 1) * half, :] = total.astype(ref.dtype)


def gather(own, received):
    rows, width = own.shape
    return pl.pallas_call(
        gather_kernel,
        out_shape=(
            held((rows // 2, width), jnp.float32),
            held((rows // 2, width), jnp.bfloat16),
        ),
        in_specs=[VMEM] * 4,
        out_specs=(VMEM, VMEM),
        compiler_params=params(2),
        cost_estimate=COST,
        name="gather",
    )(own, *received)


def guide_kernel(guidance_ref, kept_ref, other_ref, out_ref):
    strength = guidance_ref[0]
    weight = jnp.where(lax.axis_index("branch") == 0, strength, 1.0 - strength)
    kept = kept_ref[...]
    guided = weight * kept + (1.0 - weight) * other_ref[...].astype(jnp.float32)
    out_ref[...] = guided.astype(out_ref.dtype)


def guide(guidance, kept, other):
    return pl.pallas_call(
        guide_kernel,
        out_shape=jax.ShapeDtypeStruct(other.shape, jnp.bfloat16),
        in_specs=[SMEM, VMEM, VMEM],
        out_specs=VMEM,
        compiler_params=params(2),
        cost_estimate=COST,
        name="guide",
    )(guidance, kept, other)


def on_device(tokens, partners, counts, w_query, w_key, w_value, w_out, w_in, w_back, guidance):
    per_device, tok, width = tokens.shape[1:]
    x = tokens[0].reshape(per_device * tok, width)
    count = lax.axis_size("view")

    x, kv, w_half = project(x, w_key, w_value, w_out)

    near = [matched(count, 2, parity)(kv) for parity in (1, 0)]
    across = flipped("view", count, 4)(kv)
    far = (across, onward(count)(across))
    w_1 = flipped("head", 4, 1)(w_half)
    q = ask(x, w_query, x)
    bias = biases(count, partners.T, counts, x)
    state = attend(((0, 0, True),), True, False, bias, q, (kv,))
    w_32 = flipped("head", 4, 3)(stack(w_half, w_1, after=(bias, q)))
    other_core = flipped("view", count, 1)
    other = other_core(kv)
    cross = [other_core(p) for p in pick(*near, state[1])]
    state = attend(((1, 0, True), (2, 0, False), (3, 0, False)), False, False, bias, q, (other, *near), state)
    attended = attend(((4, None, True), (5, 0, False), (6, 0, False)), False, True, bias, q, (*cross, *far), state)
    w_pair = other_core(stack(w_1, w_32, after=(attended,)))

    pieces = [attended] + [flipped("head", 4, j)(attended) for j in (1, 2, 3)]
    own, *outgoing = feed(x, lay(*pieces), (w_out, w_1, w_32, w_pair), w_in, w_back)
    received = [flipped("head", 4, j)(r) for j, r in zip((1, 2, 3), outgoing)]
    kept, sent = gather(own, received)
    other = flipped("branch", 2, 1)(sent)
    return guide(guidance, kept, other).reshape(per_device, -1, width)


def solution(mesh):
    placed = (
        P("branch", "view", None, None),
        P(None, "view"),
        P("view"),
        P(None, "head"),
        P(None, "head"),
        P(None, "head"),
        P("head", None),
        P(None, "head"),
        P("head", None),
        P(),
    )
    return jax.shard_map(
        on_device,
        mesh=mesh,
        in_specs=placed,
        out_specs=P("view", ("head", "branch"), None),
        check_vma=False,
    )
```

```python
import functools

import jax
import jax.numpy as jnp
from jax import lax
from jax.experimental import pallas as pl
from jax.experimental.pallas import tpu as pltpu
from jax.sharding import PartitionSpec as P

HD = 64
ROUNDS = 8
BIASES = 16
MASKED = -1e30
LOG2E = 1.4426950408889634

NT = (((1,), (1,)), ((), ()))
VMEM = pl.BlockSpec(memory_space=pltpu.VMEM)
SMEM = pl.BlockSpec(memory_space=pltpu.SMEM)
HBM = pl.BlockSpec(memory_space=pltpu.HBM)
ANY = pl.BlockSpec(memory_space=pl.ANY)


def params(mib):
    return pltpu.CompilerParams(vmem_limit_bytes=int(mib * 1024 * 1024))


def matched(count, apart, parity):
    route = []
    for low in range(count):
        if (low // apart) % 2 == parity:
            high = (low + apart) % count
            route += [(low, high), (high, low)]
    return functools.partial(lax.ppermute, axis_name="view", perm=route)


def onward(count):
    route = [(i, (i + 8 - 4 * (i & 4)) % count) for i in range(count)]
    return functools.partial(lax.ppermute, axis_name="view", perm=route)


def flipped(axis, count, bits):
    return functools.partial(lax.ppermute, axis_name=axis, perm=[(i, i ^ bits) for i in range(count)])


def held(shape, dtype):
    return pltpu.VMEM(shape, dtype)


def outside(*arrays):
    return tuple(pltpu.with_memory_space_constraint(a, pltpu.HBM) for a in arrays)


COST = pl.CostEstimate(flops=1000, bytes_accessed=1000, transcendentals=0)


def dot(a, b):
    return jnp.dot(a, b, preferred_element_type=jnp.float32)


def chunked(source, target, sems, count):
    rows = source.shape[0] // count
    pieces = [pl.ds(i * rows, rows) for i in range(count)]
    return [pltpu.make_async_copy(source.at[p], target.at[p], sems.at[i]) for i, p in enumerate(pieces)]


def key_views(count):
    me = lax.axis_index("view")
    core = me & 1
    near, far = 2 * (me & 2) - 2, 4 - 2 * (me & 4)
    sources = (me, me + 1 - 2 * core, me + near, me - near, me - 1 + 2 * core, me + far, me - far)
    return [2 * lax.rem(s + count, count) for s in sources]


def bias_kernel(count, partners_ref, counts_ref, after_ref, bias_ref):
    row = lax.broadcasted_iota(jnp.int32, (BIASES, bias_ref.shape[1]), 0)
    keys = row & 1
    for slot, first in enumerate(key_views(count)):
        keys = keys + jnp.where(row >> 1 == slot, first, 0)
    for qv in range(2):
        used = counts_ref[0:1, qv : qv + 1]
        times = jnp.where(row == qv, 1, 0)
        for r in range(ROUNDS):
            named = jnp.where(r < used, partners_ref[qv : qv + 1, r : r + 1], -1)
            times = times + jnp.where(keys == named, 1, 0)
        bias = jnp.log2(jnp.maximum(times, 1).astype(jnp.float32))
        bias_ref[BIASES * qv : BIASES * (qv + 1)] = jnp.where(times > 0, bias, MASKED)


def biases(count, partners, counts, after):
    return pl.pallas_call(
        functools.partial(bias_kernel, count),
        out_shape=held((2 * BIASES, 2 * HD), jnp.float32),
        in_specs=[VMEM, VMEM, ANY],
        out_specs=VMEM,
        compiler_params=params(2),
        cost_estimate=COST,
        name="biases",
    )(partners, counts, after)


def project_kernel(x_hbm, wk_hbm, wv_hbm, wo_hbm, x_ref, kv_ref, half_ref, wk, wv, sems):
    half = half_ref.shape[0]
    mine = pl.ds(pl.multiple_of((lax.axis_index("view") & 1) * half, half), half)
    pairs = ((x_hbm, x_ref), (wk_hbm, wk), (wv_hbm, wv), (wo_hbm.at[mine], half_ref))
    loads = [pltpu.make_async_copy(source, target, sems.at[i]) for i, (source, target) in enumerate(pairs)]
    for copy in loads:
        copy.start()
    rows = x_ref.shape[0]
    loads[0].wait()
    loads[1].wait()
    kv_ref[:rows] = dot(x_ref[...], wk[...]).astype(jnp.bfloat16)
    loads[2].wait()
    kv_ref[rows:] = dot(x_ref[...], wv[...]).T.astype(jnp.bfloat16)
    loads[3].wait()


def project(x, w_key, w_value, w_out):
    rows, width = x.shape
    columns = w_key.shape[1]
    return pl.pallas_call(
        project_kernel,
        out_shape=(
            held(x.shape, x.dtype),
            held((rows + columns, rows), jnp.bfloat16),
            held((w_out.shape[0] // 2, w_out.shape[1]), w_out.dtype),
        ),
        in_specs=[HBM] * 4,
        out_specs=(VMEM,) * 3,
        scratch_shapes=[pltpu.VMEM((width, columns), jnp.bfloat16)] * 2 + [pltpu.SemaphoreType.DMA((4,))],
        compiler_params=params(8),
        cost_estimate=COST,
        name="project",
    )(*outside(x, w_key, w_value, w_out))


def ask_kernel(x_ref, wq_ref, after_ref, q_ref):
    q_ref[...] = (dot(x_ref[...], wq_ref[...]) * (HD ** (-0.5) * LOG2E)).astype(jnp.bfloat16)


def ask(x, w_query, after):
    return pl.pallas_call(
        ask_kernel,
        out_shape=held((x.shape[0], w_query.shape[1]), jnp.bfloat16),
        in_specs=[VMEM, VMEM, ANY],
        out_specs=VMEM,
        compiler_params=params(4),
        cost_estimate=COST,
        name="ask",
    )(x, w_query, after)


def attend_kernel(blocks, first, last, bias_ref, q_ref, *refs):
    refs, kv_refs = list(refs), []
    for _, part, _ in blocks:
        kv_refs.append(refs.pop(0) if part is not None else (refs.pop(0), refs.pop(0)))
    if not first:
        held_ref, held_tops_ref = refs[:2]
        refs = refs[2:]
    refs = refs[-1:] if last else refs[-2:]
    rows, columns = q_ref.shape
    tok, heads = rows // 2, columns // HD
    lane = lax.broadcasted_iota(jnp.int32, (tok, columns), 1)
    for qv in range(2):
        mine = slice(qv * tok, (qv + 1) * tok)
        q = q_ref[mine]
        apart = jnp.concatenate([jnp.where(lane // HD == h, q, jnp.zeros_like(q)) for h in range(heads)], axis=0)
        scores, biases, values = [], [], []
        for (slot, part, both), kv_ref in zip(blocks, kv_refs):
            base = (part or 0) * (rows + columns)
            k_ref, v_ref, v_base = (kv_ref, kv_ref, base + rows) if part is not None else (*kv_ref, 0)
            for kvw in (0, 1) if both else (qv,):
                span = slice(kvw * tok, (kvw + 1) * tok)
                keys = k_ref[base + kvw * tok : base + (kvw + 1) * tok]
                scores.append(lax.dot_general(keys, apart, NT, preferred_element_type=jnp.float32))
                row = BIASES * qv + 2 * slot + kvw
                biases.append(jnp.concatenate([bias_ref[row : row + 1]] * heads, axis=1))
                values.append(v_ref[v_base : v_base + columns, span])
        top = functools.reduce(jnp.maximum, [jnp.max(s, axis=0, keepdims=True) + b for s, b in zip(scores, biases)])
        if not first:
            old_top, old_total = held_tops_ref[2 * qv : 2 * qv + 1], held_tops_ref[2 * qv + 1 : 2 * qv + 2]
            top = jnp.maximum(top, old_top)
            scale = jnp.exp2(old_top - top)
        weights = [jnp.exp2(s - (top - b)) for s, b in zip(scores, biases)]
        total = jnp.sum(functools.reduce(jnp.add, weights), axis=0, keepdims=True)
        if not first:
            total = total + scale * old_total
        rounded = jnp.concatenate([w.astype(jnp.bfloat16) for w in weights], axis=0)
        values = jnp.concatenate(values, axis=1)
        finished = []
        for p in range(heads // 2):
            two = dot(values[2 * p * HD : 2 * (p + 1) * HD], rounded[:, 2 * p * tok : 2 * (p + 1) * tok])
            for h in (2 * p, 2 * p + 1):
                lanes = slice(h * tok, (h + 1) * tok)
                blended = two[(h - 2 * p) * HD : (h - 2 * p + 1) * HD, (h - 2 * p) * tok : (h - 2 * p + 1) * tok]
                at = slice((qv * heads + h) * HD, (qv * heads + h + 1) * HD)
                if not first:
                    blended = blended + scale[:, lanes] * held_ref[at]
                if last:
                    finished.append(blended / total[:, lanes])
                else:
                    refs[0][at] = blended
        if last:
            refs[0][mine] = jnp.concatenate(finished, axis=0).T.astype(jnp.bfloat16)
        else:
            refs[1][2 * qv : 2 * qv + 1] = top
            refs[1][2 * qv + 1 : 2 * qv + 2] = total


def attend(blocks, first, last, bias, q, kvs, state=(), *after):
    rows, columns = q.shape
    tok, heads = rows // 2, columns // HD
    if last:
        out = held((rows, columns), jnp.bfloat16)
    else:
        out = (
            held((2 * columns, tok), jnp.float32),
            held((4, heads * tok), jnp.float32),
        )
    return pl.pallas_call(
        functools.partial(attend_kernel, blocks, first, last),
        out_shape=out,
        in_specs=[VMEM] * (2 + len(kvs) + len(state)) + [ANY] * len(after),
        out_specs=VMEM if last else (VMEM, VMEM),
        compiler_params=params(16),
        cost_estimate=COST,
        name="attend",
    )(bias, q, *kvs, *state, *after)


def pick_kernel(a_ref, b_ref, *refs):
    keys_ref, values_ref = refs[-2:]
    rows = keys_ref.shape[0]
    me = lax.axis_index("view")
    first = (me & 1) != ((me >> 1) & 1)

    @pl.when(first)
    def _():
        keys_ref[...] = a_ref[:rows]
        values_ref[...] = a_ref[rows:]

    @pl.when(jnp.logical_not(first))
    def _():
        keys_ref[...] = b_ref[:rows]
        values_ref[...] = b_ref[rows:]


def pick(a, b, *after):
    return pl.pallas_call(
        pick_kernel,
        out_shape=(held((a.shape[0] // 2, a.shape[1]), a.dtype),) * 2,
        in_specs=[VMEM] * 2 + [ANY] * len(after),
        out_specs=(VMEM,) * 2,
        compiler_params=params(2),
        cost_estimate=COST,
        name="pick",
    )(a, b, *after)


def stack_kernel(pieces, *refs):
    out_ref = refs[-1]
    at = 0
    for ref in refs[:pieces]:
        out_ref[at : at + ref.shape[0]] = ref[...]
        at += ref.shape[0]


def stack(*pieces, after=()):
    return pl.pallas_call(
        functools.partial(stack_kernel, len(pieces)),
        out_shape=held((sum(p.shape[0] for p in pieces), pieces[0].shape[1]), pieces[0].dtype),
        in_specs=[VMEM] * len(pieces) + [ANY] * len(after),
        out_specs=VMEM,
        compiler_params=params(2),
        cost_estimate=COST,
        name="stack",
    )(*pieces, *after)


def turned(ref, tok, columns=slice(None)):
    head = lax.axis_index("head")
    part = tok // 4
    pieces = []
    for j in range(4):
        for view in range(2):
            start = pl.multiple_of(view * tok + jnp.bitwise_xor(head, j) * part, part)
            pieces.append(ref[pl.ds(start, part), columns])
    return jnp.concatenate(pieces, axis=0)


def lay_kernel(a0, a1, a2, a3, out_ref):
    tok = a0.shape[0] // 2
    block = a0.shape[1]
    half = block // 2
    core = lax.axis_index("view") & 1
    out_ref[:, :block] = turned(a0, tok)
    for i, a in enumerate((a1, a3, a2)):
        for k, which in enumerate((core, 1 - core)):
            at = block * (i + 1) + half * k
            out_ref[:, at : at + half] = turned(a, tok, pl.ds(pl.multiple_of(which * half, half), half))


def lay(*pieces):
    rows, columns = pieces[0].shape
    return pl.pallas_call(
        lay_kernel,
        out_shape=held((rows, 4 * columns), pieces[0].dtype),
        in_specs=[VMEM] * 4,
        out_specs=VMEM,
        compiler_params=params(4),
        cost_estimate=pl.CostEstimate(flops=20_000_000_000, bytes_accessed=1000, transcendentals=0),
        name="lay",
    )(*pieces)


def feed_kernel(x_ref, left_ref, o0, w1, w32, pair, win_ref, wback_ref, own_ref, r1, r2, r3):
    rows, width = x_ref.shape
    tok = rows // 2
    part = tok // 4
    half = w1.shape[0]
    blocks = (w1[...], w32[:half], w32[half:])
    right = [o0[...]] + [r for i, w in enumerate(blocks) for r in (w, pair[i * half : (i + 1) * half])]
    attention = dot(left_ref[...], jnp.concatenate(right, axis=0))
    y = turned(x_ref, tok).astype(jnp.float32) + attention
    normed = (y * lax.rsqrt(jnp.mean(y * y, axis=-1, keepdims=True) + 1e-06)).astype(jnp.bfloat16)
    hidden = jax.nn.gelu(dot(normed, win_ref[...])).astype(jnp.bfloat16)
    update = dot(hidden, wback_ref[...])
    own_ref[...] = attention[: 2 * part] + update[: 2 * part]
    for j, ref in ((1, r1), (2, r2), (3, r3)):
        ref[...] = update[2 * part * j : 2 * part * (j + 1)].astype(jnp.bfloat16)


def feed(x, left, w_outs, w_in, w_back):
    rows, width = x.shape
    piece = held((rows // 4, width), jnp.bfloat16)
    return pl.pallas_call(
        feed_kernel,
        out_shape=(held((rows // 4, width), jnp.float32), piece, piece, piece),
        in_specs=[VMEM] * 8,
        out_specs=(VMEM,) * 4,
        compiler_params=params(16),
        cost_estimate=COST,
        name="feed",
    )(x, left, *w_outs, w_in, w_back)


def gather_kernel(own_ref, r1, r2, r3, kept_ref, sent_ref):
    branch = lax.axis_index("branch")
    part = own_ref.shape[0] // 2
    half = part // 2
    for view in range(2):
        for side, ref in ((1 - branch, sent_ref), (branch, kept_ref)):
            rows = pl.ds(pl.multiple_of(view * part + side * half, half), half)
            total = own_ref[rows, :]
            for r in (r1, r2, r3):
                total = total + r[rows, :].astype(jnp.float32)
            ref[view * half : (view + 1) * half, :] = total.astype(ref.dtype)


def gather(own, received):
    rows, width = own.shape
    return pl.pallas_call(
        gather_kernel,
        out_shape=(
            held((rows // 2, width), jnp.float32),
            held((rows // 2, width), jnp.bfloat16),
        ),
        in_specs=[VMEM] * 4,
        out_specs=(VMEM, VMEM),
        compiler_params=params(2),
        cost_estimate=COST,
        name="gather",
    )(own, *received)


def guide_kernel(guidance_ref, kept_ref, other_ref, out_ref):
    strength = guidance_ref[0]
    weight = jnp.where(lax.axis_index("branch") == 0, strength, 1.0 - strength)
    kept = kept_ref[...]
    guided = weight * kept + (1.0 - weight) * other_ref[...].astype(jnp.float32)
    out_ref[...] = guided.astype(out_ref.dtype)


def guide(guidance, kept, other):
    return pl.pallas_call(
        guide_kernel,
        out_shape=jax.ShapeDtypeStruct(other.shape, jnp.bfloat16),
        in_specs=[SMEM, VMEM, VMEM],
        out_specs=VMEM,
        compiler_params=params(2),
        cost_estimate=COST,
        name="guide",
    )(guidance, kept, other)


def on_device(tokens, partners, counts, w_query, w_key, w_value, w_out, w_in, w_back, guidance):
    per_device, tok, width = tokens.shape[1:]
    x = tokens[0].reshape(per_device * tok, width)
    count = lax.axis_size("view")

    x, kv, w_half = project(x, w_key, w_value, w_out)

    near = [matched(count, 2, parity)(kv) for parity in (1, 0)]
    across = flipped("view", count, 4)(kv)
    far = (across, onward(count)(across))
    w_1 = flipped("head", 4, 1)(w_half)
    q = ask(x, w_query, x)
    bias = biases(count, partners.T, counts[None], x)
    state = attend(((0, 0, True),), True, False, bias, q, (kv,))
    w_32 = flipped("head", 4, 3)(stack(w_half, w_1, after=(bias, q)))
    other_core = flipped("view", count, 1)
    other = other_core(kv)
    cross = [other_core(p) for p in pick(*near, state[1])]
    state = attend(((1, 0, True), (2, 0, False), (3, 0, False)), False, False, bias, q, (other, *near), state)
    attended = attend(((4, None, True), (5, 0, False), (6, 0, False)), False, True, bias, q, (*cross, *far), state)
    w_pair = other_core(stack(w_1, w_32, after=(attended,)))

    pieces = [attended] + [flipped("head", 4, j)(attended) for j in (1, 2, 3)]
    own, *outgoing = feed(x, lay(*pieces), (w_out, w_1, w_32, w_pair), w_in, w_back)
    received = [flipped("head", 4, j)(r) for j, r in zip((1, 2, 3), outgoing)]
    kept, sent = gather(own, received)
    other = flipped("branch", 2, 1)(sent)
    return guide(guidance, kept, other).reshape(per_device, -1, width)


def solution(mesh):
    placed = (
        P("branch", "view", None, None),
        P(None, "view"),
        P("view"),
        P(None, "head"),
        P(None, "head"),
        P(None, "head"),
        P("head", None),
        P(None, "head"),
        P("head", None),
        P(),
    )
    return jax.shard_map(
        on_device,
        mesh=mesh,
        in_specs=placed,
        out_specs=P("view", ("head", "branch"), None),
        check_vma=False,
    )
```

```python
import functools

import jax
import jax.numpy as jnp
from jax import lax
from jax.experimental import pallas as pl
from jax.experimental.pallas import tpu as pltpu
from jax.sharding import PartitionSpec as P

HD = 64
ROUNDS = 8
BIASES = 16
MASKED = -1e30
LOG2E = 1.4426950408889634

NT = (((1,), (1,)), ((), ()))
VMEM = pl.BlockSpec(memory_space=pltpu.VMEM)
SMEM = pl.BlockSpec(memory_space=pltpu.SMEM)
HBM = pl.BlockSpec(memory_space=pltpu.HBM)
ANY = pl.BlockSpec(memory_space=pl.ANY)


def params(mib):
    return pltpu.CompilerParams(vmem_limit_bytes=int(mib * 1024 * 1024))


def matched(count, apart, parity):
    route = []
    for low in range(count):
        if (low // apart) % 2 == parity:
            high = (low + apart) % count
            route += [(low, high), (high, low)]
    return functools.partial(lax.ppermute, axis_name="view", perm=route)


def onward(count):
    route = [(i, (i + 8 - 4 * (i & 4)) % count) for i in range(count)]
    return functools.partial(lax.ppermute, axis_name="view", perm=route)


def flipped(axis, count, bits):
    return functools.partial(lax.ppermute, axis_name=axis, perm=[(i, i ^ bits) for i in range(count)])


def held(shape, dtype):
    return pltpu.VMEM(shape, dtype)


def outside(*arrays):
    return tuple(pltpu.with_memory_space_constraint(a, pltpu.HBM) for a in arrays)


COST = pl.CostEstimate(flops=1000, bytes_accessed=1000, transcendentals=0)


def dot(a, b):
    return jnp.dot(a, b, preferred_element_type=jnp.float32)


def chunked(source, target, sems, count):
    rows = source.shape[0] // count
    pieces = [pl.ds(i * rows, rows) for i in range(count)]
    return [pltpu.make_async_copy(source.at[p], target.at[p], sems.at[i]) for i, p in enumerate(pieces)]


def key_views(count):
    me = lax.axis_index("view")
    core = me & 1
    near, far = 2 * (me & 2) - 2, 4 - 2 * (me & 4)
    sources = (me, me + 1 - 2 * core, me + near, me - near, me - 1 + 2 * core, me + far, me - far)
    return [2 * lax.rem(s + count, count) for s in sources]


def bias_kernel(count, partners_ref, counts_ref, after_ref, bias_ref):
    row = lax.broadcasted_iota(jnp.int32, (BIASES, bias_ref.shape[1]), 0)
    keys = row & 1
    for slot, first in enumerate(key_views(count)):
        keys = keys + jnp.where(row >> 1 == slot, first, 0)
    for qv in range(2):
        used = counts_ref[0:1, qv : qv + 1]
        times = jnp.where(row == qv, 1, 0)
        for r in range(ROUNDS):
            named = jnp.where(r < used, partners_ref[qv : qv + 1, r : r + 1], -1)
            times = times + jnp.where(keys == named, 1, 0)
        bias = jnp.log2(jnp.maximum(times, 1).astype(jnp.float32))
        bias_ref[BIASES * qv : BIASES * (qv + 1)] = jnp.where(times > 0, bias, MASKED)


def biases(count, partners, counts, after):
    return pl.pallas_call(
        functools.partial(bias_kernel, count),
        out_shape=held((2 * BIASES, 2 * HD), jnp.float32),
        in_specs=[VMEM, VMEM, ANY],
        out_specs=VMEM,
        compiler_params=params(2),
        cost_estimate=COST,
        name="biases",
    )(partners, counts, after)


def project_kernel(x_hbm, wk_hbm, wv_hbm, wo_hbm, x_ref, kv_ref, half_ref, wk, wv, sems):
    half = half_ref.shape[0]
    mine = pl.ds(pl.multiple_of((lax.axis_index("view") & 1) * half, half), half)
    pairs = ((x_hbm, x_ref), (wk_hbm, wk), (wv_hbm, wv), (wo_hbm.at[mine], half_ref))
    loads = [pltpu.make_async_copy(source, target, sems.at[i]) for i, (source, target) in enumerate(pairs)]
    for copy in loads:
        copy.start()
    rows = x_ref.shape[0]
    loads[0].wait()
    loads[1].wait()
    kv_ref[:rows] = dot(x_ref[...], wk[...]).astype(jnp.bfloat16)
    loads[2].wait()
    kv_ref[rows:] = dot(x_ref[...], wv[...]).T.astype(jnp.bfloat16)
    loads[3].wait()


def project(x, w_key, w_value, w_out):
    rows, width = x.shape
    columns = w_key.shape[1]
    return pl.pallas_call(
        project_kernel,
        out_shape=(
            held(x.shape, x.dtype),
            held((rows + columns, rows), jnp.bfloat16),
            held((w_out.shape[0] // 2, w_out.shape[1]), w_out.dtype),
        ),
        in_specs=[HBM] * 4,
        out_specs=(VMEM,) * 3,
        scratch_shapes=[pltpu.VMEM((width, columns), jnp.bfloat16)] * 2 + [pltpu.SemaphoreType.DMA((4,))],
        compiler_params=params(8),
        cost_estimate=COST,
        name="project",
    )(*outside(x, w_key, w_value, w_out))


def ask_kernel(x_ref, wq_ref, after_ref, q_ref):
    q_ref[...] = (dot(x_ref[...], wq_ref[...]) * (HD ** (-0.5) * LOG2E)).astype(jnp.bfloat16)


def ask(x, w_query, after):
    return pl.pallas_call(
        ask_kernel,
        out_shape=held((x.shape[0], w_query.shape[1]), jnp.bfloat16),
        in_specs=[VMEM, VMEM, ANY],
        out_specs=VMEM,
        compiler_params=params(4),
        cost_estimate=COST,
        name="ask",
    )(x, w_query, after)


def attend_kernel(blocks, first, last, bias_ref, q_ref, *refs):
    refs, kv_refs = list(refs), []
    for _, part, _ in blocks:
        kv_refs.append(refs.pop(0) if part is not None else (refs.pop(0), refs.pop(0)))
    if not first:
        held_ref, held_tops_ref = refs[:2]
        refs = refs[2:]
    refs = refs[-1:] if last else refs[-2:]
    rows, columns = q_ref.shape
    tok, heads = rows // 2, columns // HD
    lane = lax.broadcasted_iota(jnp.int32, (tok, columns), 1)
    for qv in range(2):
        mine = slice(qv * tok, (qv + 1) * tok)
        q = q_ref[mine]
        apart = jnp.concatenate([jnp.where(lane // HD == h, q, jnp.zeros_like(q)) for h in range(heads)], axis=0)
        scores, biases, values = [], [], []
        for (slot, part, both), kv_ref in zip(blocks, kv_refs):
            base = (part or 0) * (rows + columns)
            k_ref, v_ref, v_base = (kv_ref, kv_ref, base + rows) if part is not None else (*kv_ref, 0)
            for kvw in (0, 1) if both else (qv,):
                span = slice(kvw * tok, (kvw + 1) * tok)
                keys = k_ref[base + kvw * tok : base + (kvw + 1) * tok]
                scores.append(lax.dot_general(keys, apart, NT, preferred_element_type=jnp.float32))
                row = BIASES * qv + 2 * slot + kvw
                biases.append(jnp.concatenate([bias_ref[row : row + 1]] * heads, axis=1))
                values.append(v_ref[v_base : v_base + columns, span])
        top = functools.reduce(jnp.maximum, [jnp.max(s, axis=0, keepdims=True) + b for s, b in zip(scores, biases)])
        if not first:
            old_top, old_total = held_tops_ref[2 * qv : 2 * qv + 1], held_tops_ref[2 * qv + 1 : 2 * qv + 2]
            top = jnp.maximum(top, old_top)
            scale = jnp.exp2(old_top - top)
        weights = [jnp.exp2(s - (top - b)) for s, b in zip(scores, biases)]
        total = jnp.sum(functools.reduce(jnp.add, weights), axis=0, keepdims=True)
        if not first:
            total = total + scale * old_total
        inverse = 1.0 / total
        rounded = jnp.concatenate([w.astype(jnp.bfloat16) for w in weights], axis=0)
        values = jnp.concatenate(values, axis=1)
        finished = []
        for p in range(heads // 2):
            two = dot(values[2 * p * HD : 2 * (p + 1) * HD], rounded[:, 2 * p * tok : 2 * (p + 1) * tok])
            for h in (2 * p, 2 * p + 1):
                lanes = slice(h * tok, (h + 1) * tok)
                blended = two[(h - 2 * p) * HD : (h - 2 * p + 1) * HD, (h - 2 * p) * tok : (h - 2 * p + 1) * tok]
                at = slice((qv * heads + h) * HD, (qv * heads + h + 1) * HD)
                if not first:
                    blended = blended + scale[:, lanes] * held_ref[at]
                if last:
                    finished.append(blended * inverse[:, lanes])
                else:
                    refs[0][at] = blended
        if last:
            refs[0][mine] = jnp.concatenate(finished, axis=0).T.astype(jnp.bfloat16)
        else:
            refs[1][2 * qv : 2 * qv + 1] = top
            refs[1][2 * qv + 1 : 2 * qv + 2] = total


def attend(blocks, first, last, bias, q, kvs, state=(), *after):
    rows, columns = q.shape
    tok, heads = rows // 2, columns // HD
    if last:
        out = held((rows, columns), jnp.bfloat16)
    else:
        out = (
            held((2 * columns, tok), jnp.float32),
            held((4, heads * tok), jnp.float32),
        )
    return pl.pallas_call(
        functools.partial(attend_kernel, blocks, first, last),
        out_shape=out,
        in_specs=[VMEM] * (2 + len(kvs) + len(state)) + [ANY] * len(after),
        out_specs=VMEM if last else (VMEM, VMEM),
        compiler_params=params(16),
        cost_estimate=COST,
        name="attend",
    )(bias, q, *kvs, *state, *after)


def pick_kernel(a_ref, b_ref, *refs):
    keys_ref, values_ref = refs[-2:]
    rows = keys_ref.shape[0]
    me = lax.axis_index("view")
    first = (me & 1) != ((me >> 1) & 1)

    @pl.when(first)
    def _():
        keys_ref[...] = a_ref[:rows]
        values_ref[...] = a_ref[rows:]

    @pl.when(jnp.logical_not(first))
    def _():
        keys_ref[...] = b_ref[:rows]
        values_ref[...] = b_ref[rows:]


def pick(a, b, *after):
    return pl.pallas_call(
        pick_kernel,
        out_shape=(held((a.shape[0] // 2, a.shape[1]), a.dtype),) * 2,
        in_specs=[VMEM] * 2 + [ANY] * len(after),
        out_specs=(VMEM,) * 2,
        compiler_params=params(2),
        cost_estimate=COST,
        name="pick",
    )(a, b, *after)


def stack_kernel(pieces, *refs):
    out_ref = refs[-1]
    at = 0
    for ref in refs[:pieces]:
        out_ref[at : at + ref.shape[0]] = ref[...]
        at += ref.shape[0]


def stack(*pieces, after=()):
    return pl.pallas_call(
        functools.partial(stack_kernel, len(pieces)),
        out_shape=held((sum(p.shape[0] for p in pieces), pieces[0].shape[1]), pieces[0].dtype),
        in_specs=[VMEM] * len(pieces) + [ANY] * len(after),
        out_specs=VMEM,
        compiler_params=params(2),
        cost_estimate=COST,
        name="stack",
    )(*pieces, *after)


def turned(ref, tok, columns=slice(None)):
    head = lax.axis_index("head")
    part = tok // 4
    pieces = []
    for j in range(4):
        for view in range(2):
            start = pl.multiple_of(view * tok + jnp.bitwise_xor(head, j) * part, part)
            pieces.append(ref[pl.ds(start, part), columns])
    return jnp.concatenate(pieces, axis=0)


def lay_kernel(a0, a1, a2, a3, out_ref):
    tok = a0.shape[0] // 2
    block = a0.shape[1]
    half = block // 2
    core = lax.axis_index("view") & 1
    out_ref[:, :block] = turned(a0, tok)
    for i, a in enumerate((a1, a3, a2)):
        for k, which in enumerate((core, 1 - core)):
            at = block * (i + 1) + half * k
            out_ref[:, at : at + half] = turned(a, tok, pl.ds(pl.multiple_of(which * half, half), half))


def lay(*pieces):
    rows, columns = pieces[0].shape
    return pl.pallas_call(
        lay_kernel,
        out_shape=held((rows, 4 * columns), pieces[0].dtype),
        in_specs=[VMEM] * 4,
        out_specs=VMEM,
        compiler_params=params(4),
        cost_estimate=pl.CostEstimate(flops=20_000_000_000, bytes_accessed=1000, transcendentals=0),
        name="lay",
    )(*pieces)


def feed_kernel(x_ref, left_ref, o0, w1, w32, pair, win_ref, wback_ref, own_ref, r1, r2, r3):
    rows, width = x_ref.shape
    tok = rows // 2
    part = tok // 4
    half = w1.shape[0]
    blocks = (w1[...], w32[:half], w32[half:])
    right = [o0[...]] + [r for i, w in enumerate(blocks) for r in (w, pair[i * half : (i + 1) * half])]
    attention = dot(left_ref[...], jnp.concatenate(right, axis=0))
    y = turned(x_ref, tok).astype(jnp.float32) + attention
    normed = (y * lax.rsqrt(jnp.mean(y * y, axis=-1, keepdims=True) + 1e-06)).astype(jnp.bfloat16)
    hidden = jax.nn.gelu(dot(normed, win_ref[...])).astype(jnp.bfloat16)
    update = dot(hidden, wback_ref[...])
    own_ref[...] = attention[: 2 * part] + update[: 2 * part]
    for j, ref in ((1, r1), (2, r2), (3, r3)):
        ref[...] = update[2 * part * j : 2 * part * (j + 1)].astype(jnp.bfloat16)


def feed(x, left, w_outs, w_in, w_back):
    rows, width = x.shape
    piece = held((rows // 4, width), jnp.bfloat16)
    return pl.pallas_call(
        feed_kernel,
        out_shape=(held((rows // 4, width), jnp.float32), piece, piece, piece),
        in_specs=[VMEM] * 8,
        out_specs=(VMEM,) * 4,
        compiler_params=params(16),
        cost_estimate=COST,
        name="feed",
    )(x, left, *w_outs, w_in, w_back)


def gather_kernel(own_ref, r1, r2, r3, kept_ref, sent_ref):
    branch = lax.axis_index("branch")
    part = own_ref.shape[0] // 2
    half = part // 2
    for view in range(2):
        for side, ref in ((1 - branch, sent_ref), (branch, kept_ref)):
            rows = pl.ds(pl.multiple_of(view * part + side * half, half), half)
            total = own_ref[rows, :]
            for r in (r1, r2, r3):
                total = total + r[rows, :].astype(jnp.float32)
            ref[view * half : (view + 1) * half, :] = total.astype(ref.dtype)


def gather(own, received):
    rows, width = own.shape
    return pl.pallas_call(
        gather_kernel,
        out_shape=(
            held((rows // 2, width), jnp.float32),
            held((rows // 2, width), jnp.bfloat16),
        ),
        in_specs=[VMEM] * 4,
        out_specs=(VMEM, VMEM),
        compiler_params=params(2),
        cost_estimate=COST,
        name="gather",
    )(own, *received)


def guide_kernel(guidance_ref, kept_ref, other_ref, out_ref):
    strength = guidance_ref[0]
    weight = jnp.where(lax.axis_index("branch") == 0, strength, 1.0 - strength)
    kept = kept_ref[...]
    guided = weight * kept + (1.0 - weight) * other_ref[...].astype(jnp.float32)
    out_ref[...] = guided.astype(out_ref.dtype)


def guide(guidance, kept, other):
    return pl.pallas_call(
        guide_kernel,
        out_shape=jax.ShapeDtypeStruct(other.shape, jnp.bfloat16),
        in_specs=[SMEM, VMEM, VMEM],
        out_specs=VMEM,
        compiler_params=params(2),
        cost_estimate=COST,
        name="guide",
    )(guidance, kept, other)


def on_device(tokens, partners, counts, w_query, w_key, w_value, w_out, w_in, w_back, guidance):
    per_device, tok, width = tokens.shape[1:]
    x = tokens[0].reshape(per_device * tok, width)
    count = lax.axis_size("view")

    x, kv, w_half = project(x, w_key, w_value, w_out)

    near = [matched(count, 2, parity)(kv) for parity in (1, 0)]
    across = flipped("view", count, 4)(kv)
    far = (across, onward(count)(across))
    w_1 = flipped("head", 4, 1)(w_half)
    q = ask(x, w_query, x)
    bias = biases(count, partners.T, counts[None], x)
    state = attend(((0, 0, True),), True, False, bias, q, (kv,))
    w_32 = flipped("head", 4, 3)(stack(w_half, w_1, after=(bias, q)))
    other_core = flipped("view", count, 1)
    other = other_core(kv)
    cross = [other_core(p) for p in pick(*near, state[1])]
    state = attend(((1, 0, True), (2, 0, False), (3, 0, False)), False, False, bias, q, (other, *near), state)
    attended = attend(((4, None, True), (5, 0, False), (6, 0, False)), False, True, bias, q, (*cross, *far), state)
    w_pair = other_core(stack(w_1, w_32, after=(attended,)))

    pieces = [attended] + [flipped("head", 4, j)(attended) for j in (1, 2, 3)]
    own, *outgoing = feed(x, lay(*pieces), (w_out, w_1, w_32, w_pair), w_in, w_back)
    received = [flipped("head", 4, j)(r) for j, r in zip((1, 2, 3), outgoing)]
    kept, sent = gather(own, received)
    other = flipped("branch", 2, 1)(sent)
    return guide(guidance, kept, other).reshape(per_device, -1, width)


def solution(mesh):
    placed = (
        P("branch", "view", None, None),
        P(None, "view"),
        P("view"),
        P(None, "head"),
        P(None, "head"),
        P(None, "head"),
        P("head", None),
        P(None, "head"),
        P("head", None),
        P(),
    )
    return jax.shard_map(
        on_device,
        mesh=mesh,
        in_specs=placed,
        out_specs=P("view", ("head", "branch"), None),
        check_vma=False,
    )
```
